512 devices in a mesh: section: 16 (over x, z_lo), seq: 16 (over z_hi, y), cfg: 2 (over core).
Axes of the slice: x: 4, y: 4, z: 16 (z_hi: 4, z_lo: 4; z = z_hi * 4 + z_lo), core: 2. Of those that a mesh axis runs over, the one named last changes fastest.
Arguments:
- latent: bfloat16 [64, 3072], P(None, 'seq'), may hold values from -6 to 6
- timestep: int32 [1], replicated, may hold values from 0 to 7
- modulation: bfloat16 [16, 16, 3, 3072], P('section', 'cfg'), parts along dimension 1, may hold values from -4 to 4
- qkv_weight: bfloat16 [16, 3072, 3, 2048], P('section', None, None, 'seq'), may hold values from -0.109375 to 0.109375
- out_weight: bfloat16 [16, 2048, 3072], P('section', None, 'seq'), may hold values from -0.125 to 0.125
- stale_kv: bfloat16 [16, 2, 128, 2048], P('section', None, 'cfg', 'seq'), parts along dimension 2, may hold values from -6 to 6
Outputs:
- hidden_out: bfloat16 [16, 128, 3072], P('section', 'cfg', 'seq'), parts along dimension 1
- kv_next: bfloat16 [16, 2, 128, 2048], P('section', None, 'cfg', 'seq'), parts along dimension 2
The draws below stay inside these ranges and needn't reach their ends.
There are 2 independent parts, one for each index of `cfg`. The reference program is written for one: setup_inputs(seed, part) draws one part's arguments, and reference() takes and returns one part's arrays. A program takes and returns all parts, laid end to end along the dimension named above; an argument that names none is the same for every part. Nothing has to cross between parts.
All inputs are finite; a program needn't handle non-finite values.
Results may differ from the reference program's by a relative error of at most 0.02.
Values may be sent and summed in bfloat16 or wider, within the bound.
A program may use at most 64 MiB of HBM per device.

```python
import jax
import jax.numpy as jnp
from jax import lax

D = 3072
HEAD_DIM = 128
HEADS = 16
INNER = 2048
PATCHES = 2
PATCH_TOK = 32
TOKENS = 64
TSTEPS = 8
LAYERS = 16


def level_of(own_key, extent, split, low, high):
    gain, own = 1.0, jax.random.fold_in(own_key, 6)
    for axis_at, parts in split:
        heights = jnp.exp(jax.random.uniform(jax.random.fold_in(own, axis_at), (parts,), jnp.float32, low / len(split), high / len(split)))
        gain = gain * jnp.repeat(heights, extent[axis_at] // parts).reshape([-1 if axis == axis_at else 1 for axis in range(len(extent))])
    return gain


def gaussian(rng, dims, deviation, most, pieces=(), held_as=jnp.bfloat16):
    values = deviation * jax.random.normal(rng, dims, jnp.float32)
    if pieces:
        values = values * level_of(rng, dims, pieces, -0.22, 0.18)
    return jnp.clip(values, -most, most).astype(held_as)


def setup_inputs(seed: int = 0, part: int = 0) -> dict:
    streams_of = jax.random.split(jax.random.key(seed), 7)
    own_keys = jax.random.split(jax.random.fold_in(streams_of[6], part), 7)
    latent = gaussian(streams_of[0], (TOKENS, D), 1.0, 6.0, ((1, 16),))
    timestep = jax.random.randint(streams_of[1], (1,), 0, TSTEPS).astype(jnp.int32)
    modulation = gaussian(own_keys[2], (LAYERS, TSTEPS, 3, D), 0.8, 4.0, ((0, 16),))
    qkv_weight = gaussian(streams_of[3], (LAYERS, D, 3, INNER), D ** -0.5, 0.109375, ((0, 16), (3, 16)))
    out_weight = gaussian(streams_of[4], (LAYERS, INNER, D), INNER ** -0.5, 0.125, ((0, 16), (2, 16)))
    stale_kv = gaussian(own_keys[5], (LAYERS, 2, TOKENS, INNER), 1.0, 6.0, ((0, 16), (3, 16)))
    return {"latent": latent, "timestep": timestep, "modulation": modulation, "qkv_weight": qkv_weight, "out_weight": out_weight, "stale_kv": stale_kv}


EPS_NORM = 1e-06

def norm_rows(values):
    center = lax.optimization_barrier(jnp.mean(values, axis=-1, keepdims=True))
    centred = values - center
    spread = lax.optimization_barrier(jnp.mean(centred * centred, axis=-1, keepdims=True))
    return centred / jnp.sqrt(spread + EPS_NORM)

def rms_heads(values):
    return values / jnp.sqrt(lax.optimization_barrier(jnp.mean(values * values, axis=-1, keepdims=True)) + EPS_NORM)

def reference(latent, timestep, modulation, qkv_weight, out_weight, stale_kv):
    stream = latent
    hidden_list = []
    cache_list = []
    for layer_num in range(LAYERS):
        mod_table = lax.dynamic_index_in_dim(modulation[layer_num], timestep[0], 0, keepdims=False).astype(jnp.float32)
        shift_vec, scale_vec, gate_vec = (mod_table[0], mod_table[1], mod_table[2])
        joint_weight = qkv_weight[layer_num].reshape(D, 3 * INNER)
        key_cache = stale_kv[layer_num, 0]
        value_cache = stale_kv[layer_num, 1]
        new_parts = []
        for patch_num in range(PATCHES):
            first_row = patch_num * PATCH_TOK
            patch_rows = stream[first_row:first_row + PATCH_TOK]
            normed = (norm_rows(patch_rows.astype(jnp.float32)) * (1.0 + scale_vec) + shift_vec).astype(jnp.bfloat16)
            projected = jnp.dot(normed, joint_weight, preferred_element_type=jnp.float32)
            projected = projected.reshape(PATCH_TOK, 3, HEADS, HEAD_DIM)
            query_rows = rms_heads(projected[:, 0]).astype(jnp.bfloat16)
            key_rows = rms_heads(projected[:, 1]).astype(jnp.bfloat16).reshape(PATCH_TOK, INNER)
            value_rows = projected[:, 2].astype(jnp.bfloat16).reshape(PATCH_TOK, INNER)
            key_cache = key_cache.at[first_row:first_row + PATCH_TOK].set(key_rows)
            value_cache = value_cache.at[first_row:first_row + PATCH_TOK].set(value_rows)
            scores = jnp.einsum('phd,thd->hpt', query_rows.astype(jnp.float32), key_cache.reshape(TOKENS, HEADS, HEAD_DIM).astype(jnp.float32)) * HEAD_DIM ** (-0.5)
            exponent = jnp.exp(scores)
            weights_soft = (exponent / lax.optimization_barrier(jnp.sum(exponent, axis=-1, keepdims=True))).astype(jnp.bfloat16)
            attended = jnp.einsum('hpt,thd->phd', weights_soft.astype(jnp.float32), value_cache.reshape(TOKENS, HEADS, HEAD_DIM).astype(jnp.float32))
            attended = attended.astype(jnp.bfloat16).reshape(PATCH_TOK, INNER)
            update = jnp.dot(attended, out_weight[layer_num], preferred_element_type=jnp.float32)
            new_parts.append((patch_rows.astype(jnp.float32) + gate_vec * update).astype(jnp.bfloat16))
        stream = jnp.concatenate(new_parts, axis=0)
        hidden_list.append(stream)
        cache_list.append(jnp.stack([key_cache, value_cache]))
    return (jnp.stack(hidden_list), jnp.stack(cache_list))
```

```python
import jax
import jax.numpy as jnp
from jax import lax
from jax.experimental import pallas as pl
from jax.experimental.pallas import tpu as pltpu
from jax.sharding import PartitionSpec as P

D = 3072
HEAD_DIM = 128
INNER = 2048
PATCHES = 2
PATCH_TOK = 32
TOKENS = 64
WIDTH = 192
ZS = 4
YS = 4
SEQ = 16
LAYERS = 16
EPS_NORM = 1e-06
MESH = pl.DeviceIdType.MESH


def kernel(
    t_ref, latent, mod, wq, wo, stale,
    hid_out, kv_out,
    wbuf, wobuf, modbuf, vecs, cache, hb, att, own, nrm,
    ld_sem, h_send, h_recv, a_send, a_recv,
):
    sec = lax.axis_index("section")
    me = lax.axis_index("seq")
    cfg = lax.axis_index("cfg")
    zh = me // YS
    y = lax.rem(me, YS)

    loads = [
        pltpu.make_async_copy(mod, modbuf, ld_sem.at[0]),
        pltpu.make_async_copy(stale, cache, ld_sem.at[1]),
        pltpu.make_async_copy(latent, own, ld_sem.at[2]),
        pltpu.make_async_copy(wo, wobuf, ld_sem.at[3]),
    ]
    for part in range(3):
        for col in range(YS):
            loads.append(
                pltpu.make_async_copy(
                    wq.at[part, :, col],
                    wbuf.at[col, :, :, pl.ds(part * HEAD_DIM, HEAD_DIM)],
                    ld_sem.at[4 + part * YS + col],
                )
            )
    for one in loads:
        one.start()

    barrier = pltpu.get_barrier_semaphore()

    def greet_own(j, _):
        pl.semaphore_signal(
            barrier, inc=1, device_id=(sec, lax.rem(me + j, SEQ), cfg), device_id_type=MESH
        )
        return 0

    lax.fori_loop(1, SEQ, greet_own, 0)

    @pl.when(sec > 0)
    def _():
        def greet_before(j, _):
            pl.semaphore_signal(
                barrier, inc=1, device_id=(sec - 1, j, cfg), device_id_type=MESH
            )
            return 0

        lax.fori_loop(0, SEQ, greet_before, 0)

    loads[0].wait()
    pick = lax.broadcasted_iota(jnp.int32, (8, D), 0) == t_ref[0]
    for part in range(3):
        row = jnp.sum(
            jnp.where(pick, modbuf[part].astype(jnp.float32), 0.0), axis=0, keepdims=True
        )
        row = jnp.concatenate(
            [
                row[:, (z * YS + col) * WIDTH : (z * YS + col + 1) * WIDTH]
                for col in range(YS)
                for z in range(ZS)
            ],
            axis=1,
        )
        vecs[part] = row + 1.0 if part == 1 else row
    loads[1].wait()
    loads[2].wait()

    @pl.when(sec < LAYERS - 1)
    def _():
        pl.semaphore_wait(barrier, 2 * SEQ - 1)

    @pl.when(sec == LAYERS - 1)
    def _():
        pl.semaphore_wait(barrier, SEQ - 1)

    def rows(patch):
        return pl.ds(patch * PATCH_TOK, PATCH_TOK)

    def h_copy(patch, section, to):
        return pltpu.make_async_remote_copy(
            src_ref=own.at[rows(patch)],
            dst_ref=hb.at[patch, me],
            send_sem=h_send.at[patch, to],
            recv_sem=h_recv.at[patch, me],
            device_id=(section, to, cfg),
            device_id_type=MESH,
        )

    def a_copy(patch, to):
        mine = att.at[patch, zh, :, pl.ds(pl.multiple_of(y * HEAD_DIM, HEAD_DIM), HEAD_DIM)]
        return pltpu.make_async_remote_copy(
            src_ref=mine,
            dst_ref=mine,
            send_sem=a_send.at[patch, to],
            recv_sem=a_recv.at[patch, me],
            device_id=(sec, to, cfg),
            device_id_type=MESH,
        )

    def a_landing(patch, source):
        place = att.at[
            patch,
            source // YS,
            :,
            pl.ds(pl.multiple_of(lax.rem(source, YS) * HEAD_DIM, HEAD_DIM), HEAD_DIM),
        ]
        return pltpu.make_async_remote_copy(
            src_ref=place,
            dst_ref=place,
            send_sem=a_send.at[patch, source],
            recv_sem=a_recv.at[patch, source],
            device_id=(sec, source, cfg),
            device_id_type=MESH,
        )

    def h_landing(patch, source):
        return pltpu.make_async_remote_copy(
            src_ref=own.at[rows(patch)],
            dst_ref=hb.at[patch, source],
            send_sem=h_send.at[patch, source],
            recv_sem=h_recv.at[patch, source],
            device_id=(sec, source, cfg),
            device_id_type=MESH,
        )

    def each_peer(act, with_self):
        for dz in (2, 1, 3, 0):
            def one(j, _, dz=dz):
                act(lax.rem(zh + dz, ZS) * YS + lax.rem(y + j, YS))
                return 0

            lax.fori_loop(1 if dz == 0 and not with_self else 0, YS, one, 0)

    @pl.when(sec == 0)
    def _():
        for patch in range(PATCHES):
            each_peer(lambda to: h_copy(patch, sec, to).start(), False)
            hb[patch, me] = own[rows(patch)]
        for patch in range(PATCHES):
            each_peer(lambda to: h_landing(patch, to).wait_recv(), False)
        for patch in range(PATCHES):
            each_peer(lambda to: h_copy(patch, sec, to).wait_send(), False)

    def front(patch):
        @pl.when(sec > 0)
        def _():
            each_peer(lambda to: h_landing(patch, to).wait_recv(), True)

        whole = jnp.concatenate(
            [
                hb[patch, z * YS + col].astype(jnp.float32)
                for col in range(YS)
                for z in range(ZS)
            ],
            axis=1,
        )
        centred = whole - jnp.mean(whole, axis=-1, keepdims=True)
        spread = jnp.mean(centred * centred, axis=-1, keepdims=True)
        nrm[...] = (
            centred * (1.0 / jnp.sqrt(spread + EPS_NORM)) * vecs[1] + vecs[0]
        ).astype(jnp.bfloat16)
        if patch == 0:
            for one in loads[4:]:
                one.wait()
        projected = jnp.dot(
            nrm[...], wbuf[...].reshape(D, 3 * HEAD_DIM), preferred_element_type=jnp.float32
        )

        def rms(values):
            square = jnp.mean(values * values, axis=-1, keepdims=True)
            return (values * (1.0 / jnp.sqrt(square + EPS_NORM))).astype(jnp.bfloat16)

        query = rms(projected[:, :HEAD_DIM])
        cache[0, rows(patch), :] = rms(projected[:, HEAD_DIM : 2 * HEAD_DIM])
        cache[1, rows(patch), :] = projected[:, 2 * HEAD_DIM :].astype(jnp.bfloat16)
        scores = lax.dot_general(
            query, cache[0], (((1,), (1,)), ((), ())), preferred_element_type=jnp.float32
        )
        exponent = jnp.exp(scores * HEAD_DIM ** (-0.5))
        probs = (exponent * (1.0 / jnp.sum(exponent, axis=-1, keepdims=True))).astype(
            jnp.bfloat16
        )
        attended = jnp.dot(probs, cache[1], preferred_element_type=jnp.float32)
        att[
            patch, zh, :, pl.ds(pl.multiple_of(y * HEAD_DIM, HEAD_DIM), HEAD_DIM)
        ] = attended.astype(jnp.bfloat16)
        each_peer(lambda to: a_copy(patch, to).start(), False)

    def back(patch):
        if patch == 0:
            loads[3].wait()
        mine = vecs[2, :, pl.ds(pl.multiple_of(y * ZS * WIDTH, ZS * WIDTH), ZS * WIDTH)]
        gate = jnp.zeros((1, WIDTH), jnp.float32)
        for z in range(ZS):
            gate = gate + jnp.where(zh == z, mine[:, z * WIDTH : (z + 1) * WIDTH], 0.0)
        each_peer(lambda to: a_landing(patch, to).wait_recv(), False)
        update = jnp.zeros((PATCH_TOK, WIDTH), jnp.float32)
        for z in range(ZS):
            update = update + lax.dot_general(
                att[patch, z],
                wobuf[:, z * YS * HEAD_DIM : (z + 1) * YS * HEAD_DIM],
                (((1,), (1,)), ((), ())),
                preferred_element_type=jnp.float32,
            )
        result = (hb[patch, me].astype(jnp.float32) + gate * update).astype(jnp.bfloat16)
        own[rows(patch)] = result
        hid_out[rows(patch), :] = result

        @pl.when(sec < LAYERS - 1)
        def _():
            each_peer(lambda to: h_copy(patch, sec + 1, to).start(), True)

    for patch in range(PATCHES):
        front(patch)
    for patch in range(PATCHES):
        back(patch)
    kv_out[...] = cache[...]
    for patch in range(PATCHES):
        each_peer(lambda to: a_copy(patch, to).wait_send(), False)

        @pl.when(sec < LAYERS - 1)
        def _():
            each_peer(lambda to: h_copy(patch, sec + 1, to).wait_send(), True)


def on_device(latent, timestep, modulation, qkv_weight, out_weight, stale_kv):
    any_space = pl.BlockSpec(memory_space=pl.ANY)
    in_vmem = pl.BlockSpec(memory_space=pltpu.VMEM)
    bf16 = jnp.bfloat16
    hidden, caches = pl.pallas_call(
        kernel,
        out_shape=(
            jax.ShapeDtypeStruct((TOKENS, WIDTH), bf16),
            jax.ShapeDtypeStruct((2, TOKENS, HEAD_DIM), bf16),
        ),
        in_specs=[pl.BlockSpec(memory_space=pltpu.SMEM)] + [any_space] * 5,
        out_specs=(in_vmem, in_vmem),
        scratch_shapes=[
            pltpu.VMEM((YS, ZS, WIDTH, 3 * HEAD_DIM), bf16),
            pltpu.VMEM((WIDTH, INNER), bf16),
            pltpu.VMEM((3, 8, D), bf16),
            pltpu.VMEM((3, 1, D), jnp.float32),
            pltpu.VMEM((2, TOKENS, HEAD_DIM), bf16),
            pltpu.VMEM((PATCHES, SEQ, PATCH_TOK, WIDTH), bf16),
            pltpu.VMEM((PATCHES, ZS, PATCH_TOK, YS * HEAD_DIM), bf16),
            pltpu.VMEM((TOKENS, WIDTH), bf16),
            pltpu.VMEM((PATCH_TOK, D), bf16),
            pltpu.SemaphoreType.DMA((16,)),
            pltpu.SemaphoreType.DMA((PATCHES, SEQ)),
            pltpu.SemaphoreType.DMA((PATCHES, SEQ)),
            pltpu.SemaphoreType.DMA((PATCHES, SEQ)),
            pltpu.SemaphoreType.DMA((PATCHES, SEQ)),
        ],
        compiler_params=pltpu.CompilerParams(
            collective_id=0, has_side_effects=True, vmem_limit_bytes=48 * 1024 * 1024
        ),
    )(
        timestep,
        latent,
        modulation[0].transpose(1, 0, 2),
        qkv_weight[0].transpose(1, 0, 2).reshape(3, ZS, YS, WIDTH, HEAD_DIM),
        out_weight[0].transpose(1, 0),
        stale_kv[0],
    )
    return hidden[None], caches[None]


def solution(mesh):
    placed = (
        P(None, "seq"),
        P(),
        P("section", "cfg", None, None),
        P("section", None, None, "seq"),
        P("section", None, "seq"),
        P("section", None, "cfg", "seq"),
    )
    return jax.shard_map(
        on_device,
        mesh=mesh,
        in_specs=placed,
        out_specs=(P("section", "cfg", "seq"), P("section", None, "cfg", "seq")),
        check_vma=False,
    )
```

```python
import jax
import jax.numpy as jnp
from jax import lax
from jax.experimental import pallas as pl
from jax.experimental.pallas import tpu as pltpu
from jax.sharding import PartitionSpec as P

D = 3072
HEAD_DIM = 128
INNER = 2048
PATCHES = 2
PATCH_TOK = 32
TOKENS = 64
WIDTH = 192
ZS = 4
YS = 4
SEQ = 16
LAYERS = 16
GROUP = ZS * HEAD_DIM
WIDE = ZS * WIDTH
EPS_NORM = 1e-06
MESH = pl.DeviceIdType.MESH

FIRST = 2
HOST = (0, 0, 0, 1, 2, 3, 0, 1, 2, 2, 3, 3, 0, 0, 1, 1)
CHUNKS = 3 * YS + 1


def host_of(section):
    place = section * 0
    for layer in range(LAYERS):
        if HOST[layer]:
            place = jnp.where(section == layer, HOST[layer], place)
    return place


def kernel(
    t_ref, latent, mod, wq, wo, stale,
    hid_out, kv_out,
    wbuf, wobuf, modbuf, vecs, cache, hb, hwide, att, own, wide, hst, hland, kvland, nrm,
    ld_sem, h_send, h_recv, a_send, a_recv,
    w_send, w_recv, f_send, f_recv, s_send, s_recv, o_send, o_recv,
):
    sec = lax.axis_index("section")
    me = lax.axis_index("seq")
    cfg = lax.axis_index("cfg")
    zh = me // YS
    y = lax.rem(me, YS)
    place = host_of(sec)
    spread = sec < FIRST
    hosting = (sec >= FIRST) & (zh == place)
    helping = (sec >= FIRST) & (zh != place)

    def rows(patch):
        return pl.ds(patch * PATCH_TOK, PATCH_TOK)

    def lanes(number, size=HEAD_DIM):
        return pl.ds(pl.multiple_of(number * size, size), size)

    def remote(src, dst, send, recv, device):
        return pltpu.make_async_remote_copy(
            src_ref=src, dst_ref=dst, send_sem=send, recv_sem=recv,
            device_id=device, device_id_type=MESH,
        )

    def greet(device):
        pl.semaphore_signal(barrier, inc=1, device_id=device, device_id_type=MESH)

    def loop(low, high, act):
        def one(j, _):
            act(j)
            return 0

        lax.fori_loop(low, high, one, 0)

    def each_peer(act, with_self):
        for dz in (2, 1, 3, 0):
            loop(
                1 if dz == 0 and not with_self else 0,
                YS,
                lambda j, dz=dz: act(lax.rem(zh + dz, ZS) * YS + lax.rem(y + j, YS)),
            )

    def each_ring(act, with_self):
        for dy in (2, 1, 3, 0) if with_self else (2, 1, 3):
            act(lax.rem(y + dy, YS))

    def each_helper(act):
        loop(1, ZS, lambda j: act(lax.rem(place + j, ZS)))

    loads = [
        pltpu.make_async_copy(mod, modbuf, ld_sem.at[0]),
        pltpu.make_async_copy(stale, cache.at[zh], ld_sem.at[1]),
        pltpu.make_async_copy(latent, own, ld_sem.at[2]),
        pltpu.make_async_copy(
            wo, wobuf.at[pl.ds(pl.multiple_of(zh * WIDTH, WIDTH), WIDTH)], ld_sem.at[3]
        ),
    ]
    for part in range(3):
        for col in range(YS):
            loads.append(
                pltpu.make_async_copy(
                    wq.at[part, :, col],
                    wbuf.at[col, :, :, lanes(part * ZS + zh)],
                    ld_sem.at[4 + part * YS + col],
                )
            )

    @pl.when(jnp.logical_not(helping))
    def _():
        for one in loads:
            one.start()

    barrier = pltpu.get_barrier_semaphore()

    @pl.when(spread)
    def _():
        each_peer(lambda to: greet((sec, to, cfg)), False)

        @pl.when(sec > 0)
        def _():
            loop(0, SEQ, lambda j: greet((sec - 1, j, cfg)))

    @pl.when(hosting)
    def _():
        each_helper(lambda z: greet((sec, z * YS + y, cfg)))
        greet((sec, me, 1 - cfg))
        each_ring(lambda col: greet((sec, place * YS + col, cfg)), False)

        @pl.when(sec == FIRST)
        def _():
            loop(0, SEQ, lambda j: greet((sec - 1, j, cfg)))

        @pl.when(sec > FIRST)
        def _():
            before = host_of(sec - 1) * YS
            loop(0, YS, lambda j: greet((sec - 1, before + j, cfg)))

    @pl.when(helping)
    def _():
        greet((sec, place * YS + y, cfg))
        pl.semaphore_wait(barrier, 1)

    @pl.when(sec < FIRST - 1)
    def _():
        pl.semaphore_wait(barrier, SEQ - 1 + SEQ)

    @pl.when(sec == FIRST - 1)
    def _():
        pl.semaphore_wait(barrier, SEQ - 1 + YS)

    @pl.when(hosting & (sec < LAYERS - 1))
    def _():
        pl.semaphore_wait(barrier, 2 * YS - 1 + ZS)

    @pl.when(hosting & (sec == LAYERS - 1))
    def _():
        pl.semaphore_wait(barrier, YS - 1 + ZS)

    def chunk_at(number, half, z):
        if number == CHUNKS - 1:
            return wobuf.at[
                pl.ds(pl.multiple_of(z * WIDTH, WIDTH), WIDTH), lanes(half, INNER // 2)
            ]
        part, col = divmod(number, YS)
        return wbuf.at[col, pl.ds(half * 2, 2), :, lanes(part * ZS + z)]

    def chunk_from(number, half):
        if number == CHUNKS - 1:
            return wo.at[:, lanes(half, INNER // 2)]
        part, col = divmod(number, YS)
        return wq.at[part, pl.ds(half * 2, 2), col]

    def w_copy(number):
        return remote(
            chunk_from(number, cfg), chunk_at(number, cfg, zh),
            w_send.at[number], w_recv.at[zh, number], (sec, place * YS + y, cfg),
        )

    def w_landing(number, z):
        spot = chunk_at(number, cfg, z)
        return remote(
            spot, spot, w_send.at[number], w_recv.at[z, number], (sec, z * YS + y, cfg)
        )

    def swap(number, z, half):
        spot = chunk_at(number, half, z)
        return remote(
            spot, spot, f_send.at[z, number], f_recv.at[z, number], (sec, me, 1 - cfg)
        )

    def s_copy():
        return remote(
            stale, cache.at[zh], s_send, s_recv.at[zh], (sec, place * YS + y, cfg)
        )

    def s_landing(z):
        return remote(
            stale, cache.at[z], s_send, s_recv.at[z], (sec, z * YS + y, cfg)
        )

    def o_copy(z, number):
        src = cache.at[z] if number == 2 else hst.at[z, rows(number)]
        dst = kvland if number == 2 else hland.at[rows(number)]
        return remote(src, dst, o_send.at[z, number], o_recv.at[number], (sec, z * YS + y, cfg))

    @pl.when(helping)
    def _():
        s_copy().start()
        for number in range(CHUNKS):
            w_copy(number).start()
        for number in range(CHUNKS):
            w_copy(number).wait_send()
        s_copy().wait_send()
        for number in range(3):
            o_copy(zh, number).wait_recv()
        hid_out[...] = hland[...]
        kv_out[...] = kvland[...]

    def h_copy(patch, section, to):
        return remote(
            own.at[rows(patch)], hb.at[patch, me],
            h_send.at[patch, to], h_recv.at[patch, me], (section, to, cfg),
        )

    def h_landing(patch, source):
        return remote(
            own.at[rows(patch)], hb.at[patch, source],
            h_send.at[patch, source], h_recv.at[patch, source], (sec, source, cfg),
        )

    def wide_copy(patch, to, col):
        return remote(
            wide.at[patch], hwide.at[patch, y],
            h_send.at[patch, col], h_recv.at[patch, y], (sec + 1, to * YS + col, cfg),
        )

    def wide_landing(patch, col):
        return remote(
            wide.at[patch], hwide.at[patch, col],
            h_send.at[patch, col], h_recv.at[patch, col], (sec, col, cfg),
        )

    def a_copy(patch, source, to):
        spot = att.at[patch, source // YS, :, lanes(lax.rem(source, YS))]
        return remote(
            spot, spot, a_send.at[patch, to], a_recv.at[patch, source], (sec, to, cfg)
        )

    def ring_copy(patch, source, to):
        spot = att.at[patch, :, :, lanes(source)]
        return remote(
            spot, spot, a_send.at[patch, to], a_recv.at[patch, source],
            (sec, place * YS + to, cfg),
        )

    def rms(values):
        square = jnp.mean(values * values, axis=-1, keepdims=True)
        return (values * (1.0 / jnp.sqrt(square + EPS_NORM))).astype(jnp.bfloat16)

    def modulation_rows():
        loads[0].wait()
        pick = lax.broadcasted_iota(jnp.int32, (8, D), 0) == t_ref[0]
        for part in range(3):
            row = jnp.sum(
                jnp.where(pick, modbuf[part].astype(jnp.float32), 0.0), axis=0, keepdims=True
            )
            row = jnp.concatenate(
                [
                    row[:, (z * YS + col) * WIDTH : (z * YS + col + 1) * WIDTH]
                    for col in range(YS)
                    for z in range(ZS)
                ],
                axis=1,
            )
            vecs[part] = row + 1.0 if part == 1 else row

    def assemble(patch):
        for col in range(YS):
            hwide[patch, col] = jnp.concatenate(
                [hb[patch, z * YS + col].astype(jnp.float32) for z in range(ZS)], axis=1
            ).astype(jnp.bfloat16)

    def normalise(patch):
        whole = jnp.concatenate(
            [hwide[patch, col].astype(jnp.float32) for col in range(YS)], axis=1
        )
        centred = whole - jnp.mean(whole, axis=-1, keepdims=True)
        spread_of = jnp.mean(centred * centred, axis=-1, keepdims=True)
        nrm[...] = (
            centred * (1.0 / jnp.sqrt(spread_of + EPS_NORM)) * vecs[1] + vecs[0]
        ).astype(jnp.bfloat16)

    def attend(patch, z, query, key, value):
        cache[z, 0, rows(patch), :] = rms(key)
        cache[z, 1, rows(patch), :] = value.astype(jnp.bfloat16)
        scores = lax.dot_general(
            rms(query), cache[z, 0], (((1,), (1,)), ((), ())),
            preferred_element_type=jnp.float32,
        )
        exponent = jnp.exp(scores * HEAD_DIM ** (-0.5))
        probs = (exponent * (1.0 / jnp.sum(exponent, axis=-1, keepdims=True))).astype(
            jnp.bfloat16
        )
        attended = jnp.dot(probs, cache[z, 1], preferred_element_type=jnp.float32)
        att[patch, z, :, lanes(y)] = attended.astype(jnp.bfloat16)

    def project_out(patch, weight):
        update = None
        for z in range(ZS):
            term = lax.dot_general(
                att[patch, z], weight(z), (((1,), (1,)), ((), ())),
                preferred_element_type=jnp.float32,
            )
            update = term if update is None else update + term
        return update

    @pl.when(spread)
    def _():
        modulation_rows()
        loads[1].wait()
        loads[2].wait()

        @pl.when(sec == 0)
        def _():
            for patch in range(PATCHES):
                each_peer(lambda to: h_copy(patch, sec, to).start(), False)
                hb[patch, me] = own[rows(patch)]
            for patch in range(PATCHES):
                each_peer(lambda to: h_landing(patch, to).wait_recv(), False)
            for patch in range(PATCHES):
                each_peer(lambda to: h_copy(patch, sec, to).wait_send(), False)

        def front(patch):
            @pl.when(sec > 0)
            def _():
                each_peer(lambda to: h_landing(patch, to).wait_recv(), True)

            assemble(patch)
            normalise(patch)
            if patch == 0:
                for one in loads[4:]:
                    one.wait()
            projected = [
                jnp.dot(
                    nrm[...],
                    wbuf[:, :, :, lanes(part * ZS + zh)].reshape(D, HEAD_DIM),
                    preferred_element_type=jnp.float32,
                )
                for part in range(3)
            ]
            attend(patch, zh, *projected)
            each_peer(lambda to: a_copy(patch, me, to).start(), False)

        def back(patch):
            if patch == 0:
                loads[3].wait()
            mine = vecs[2, :, lanes(y, WIDE)]
            gate = jnp.zeros((1, WIDTH), jnp.float32)
            for z in range(ZS):
                gate = gate + jnp.where(zh == z, mine[:, z * WIDTH : (z + 1) * WIDTH], 0.0)
            each_peer(lambda to: a_copy(patch, to, to).wait_recv(), False)
            part = pl.ds(pl.multiple_of(zh * WIDTH, WIDTH), WIDTH)
            update = project_out(patch, lambda z: wobuf[part, z * GROUP : (z + 1) * GROUP])
            result = (hb[patch, me].astype(jnp.float32) + gate * update).astype(jnp.bfloat16)
            own[rows(patch)] = result

            @pl.when(sec < FIRST - 1)
            def _():
                each_peer(lambda to: h_copy(patch, sec + 1, to).start(), True)

            @pl.when(sec == FIRST - 1)
            def _():
                each_ring(
                    lambda col: h_copy(patch, sec + 1, HOST[FIRST] * YS + col).start(), True
                )

            hid_out[rows(patch), :] = result

        for patch in range(PATCHES):
            front(patch)
        for patch in range(PATCHES):
            back(patch)
        kv_out[...] = cache[zh]
        for patch in range(PATCHES):
            each_peer(lambda to: a_copy(patch, me, to).wait_send(), False)

            @pl.when(sec < FIRST - 1)
            def _():
                each_peer(lambda to: h_copy(patch, sec + 1, to).wait_send(), True)

            @pl.when(sec == FIRST - 1)
            def _():
                each_ring(
                    lambda col: h_copy(patch, sec + 1, HOST[FIRST] * YS + col).wait_send(), True
                )

    @pl.when(hosting)
    def _():
        modulation_rows()
        for one in loads[1:]:
            one.wait()
        for number in range(CHUNKS):
            def relay(z, number=number):
                w_landing(number, z).wait_recv()
                swap(number, z, cfg).start()

            each_helper(relay)
        each_helper(lambda z: s_landing(z).wait_recv())
        for number in range(CHUNKS):
            each_helper(lambda z: swap(number, z, 1 - cfg).wait_recv())
            each_helper(lambda z: swap(number, z, cfg).wait_send())
        after = host_of(sec + 1)

        def front(patch):
            @pl.when(sec == FIRST)
            def _():
                loop(0, SEQ, lambda j: h_landing(patch, j).wait_recv())
                assemble(patch)

            @pl.when(sec > FIRST)
            def _():
                loop(0, YS, lambda j: wide_landing(patch, j).wait_recv())

            normalise(patch)
            projected = jnp.dot(
                nrm[...], wbuf[...].reshape(D, 3 * GROUP), preferred_element_type=jnp.float32
            )
            for z in range(ZS):
                attend(
                    patch, z,
                    *[
                        projected[:, part * GROUP + z * HEAD_DIM : part * GROUP + (z + 1) * HEAD_DIM]
                        for part in range(3)
                    ],
                )
            each_ring(lambda col: ring_copy(patch, y, col).start(), False)

        def back(patch):
            each_ring(lambda col: ring_copy(patch, col, col).wait_recv(), False)
            update = project_out(patch, lambda z: wobuf[:, z * GROUP : (z + 1) * GROUP])
            result = hwide[patch, y].astype(jnp.float32) + vecs[2, :, lanes(y, WIDE)] * update
            wide[patch] = result.astype(jnp.bfloat16)

            @pl.when(sec < LAYERS - 1)
            def _():
                each_ring(lambda col: wide_copy(patch, after, col).start(), True)

            for z in range(ZS):
                hst[z, rows(patch)] = result[:, z * WIDTH : (z + 1) * WIDTH].astype(jnp.bfloat16)
            each_helper(lambda z: o_copy(z, patch).start())

        for patch in range(PATCHES):
            front(patch)
        each_helper(lambda z: o_copy(z, 2).start())
        for patch in range(PATCHES):
            back(patch)
        kv_out[...] = cache[place]
        hid_out[...] = hst[place]
        for patch in range(PATCHES):
            each_ring(lambda col: ring_copy(patch, y, col).wait_send(), False)

            @pl.when(sec < LAYERS - 1)
            def _():
                each_ring(lambda col: wide_copy(patch, after, col).wait_send(), True)

        for number in range(3):
            each_helper(lambda z: o_copy(z, number).wait_send())


def on_device(latent, timestep, modulation, qkv_weight, out_weight, stale_kv):
    any_space = pl.BlockSpec(memory_space=pl.ANY)
    in_vmem = pl.BlockSpec(memory_space=pltpu.VMEM)
    bf16 = jnp.bfloat16
    dma = pltpu.SemaphoreType.DMA
    hidden, caches = pl.pallas_call(
        kernel,
        out_shape=(
            jax.ShapeDtypeStruct((TOKENS, WIDTH), bf16),
            jax.ShapeDtypeStruct((2, TOKENS, HEAD_DIM), bf16),
        ),
        in_specs=[pl.BlockSpec(memory_space=pltpu.SMEM)] + [any_space] * 5,
        out_specs=(in_vmem, in_vmem),
        scratch_shapes=[
            pltpu.VMEM((YS, ZS, WIDTH, 3 * GROUP), bf16),
            pltpu.VMEM((WIDE, INNER), bf16),
            pltpu.VMEM((3, 8, D), bf16),
            pltpu.VMEM((3, 1, D), jnp.float32),
            pltpu.VMEM((ZS, 2, TOKENS, HEAD_DIM), bf16),
            pltpu.VMEM((PATCHES, SEQ, PATCH_TOK, WIDTH), bf16),
            pltpu.VMEM((PATCHES, YS, PATCH_TOK, WIDE), bf16),
            pltpu.VMEM((PATCHES, ZS, PATCH_TOK, YS * HEAD_DIM), bf16),
            pltpu.VMEM((TOKENS, WIDTH), bf16),
            pltpu.VMEM((PATCHES, PATCH_TOK, WIDE), bf16),
            pltpu.VMEM((ZS, TOKENS, WIDTH), bf16),
            pltpu.VMEM((TOKENS, WIDTH), bf16),
            pltpu.VMEM((2, TOKENS, HEAD_DIM), bf16),
            pltpu.VMEM((PATCH_TOK, D), bf16),
            dma((16,)),
            dma((PATCHES, SEQ)),
            dma((PATCHES, SEQ)),
            dma((PATCHES, SEQ)),
            dma((PATCHES, SEQ)),
            dma((CHUNKS,)),
            dma((ZS, CHUNKS)),
            dma((ZS, CHUNKS)),
            dma((ZS, CHUNKS)),
            dma,
            dma((ZS,)),
            dma((ZS, 3)),
            dma((3,)),
        ],
        compiler_params=pltpu.CompilerParams(
            collective_id=0, has_side_effects=True, vmem_limit_bytes=60 * 1024 * 1024
        ),
    )(
        timestep,
        latent,
        modulation[0].transpose(1, 0, 2),
        qkv_weight[0].transpose(1, 0, 2).reshape(3, ZS, YS, WIDTH, HEAD_DIM),
        out_weight[0].transpose(1, 0),
        stale_kv[0],
    )
    return hidden[None], caches[None]


def solution(mesh):
    placed = (
        P(None, "seq"),
        P(),
        P("section", "cfg", None, None),
        P("section", None, None, "seq"),
        P("section", None, "seq"),
        P("section", None, "cfg", "seq"),
    )
    return jax.shard_map(
        on_device,
        mesh=mesh,
        in_specs=placed,
        out_specs=(P("section", "cfg", "seq"), P("section", None, "cfg", "seq")),
        check_vma=False,
    )
```

```python
import jax
import jax.numpy as jnp
from jax import lax
from jax.experimental import pallas as pl
from jax.experimental.pallas import tpu as pltpu
from jax.sharding import PartitionSpec as P

D = 3072
HEAD_DIM = 128
INNER = 2048
PATCHES = 2
PATCH_TOK = 32
TOKENS = 64
WIDTH = 192
ZS = 4
YS = 4
SEQ = 16
LAYERS = 16
GROUP = ZS * HEAD_DIM
WIDE = ZS * WIDTH
EPS_NORM = 1e-06
MESH = pl.DeviceIdType.MESH

FIRST = 5
HOST = (0, 0, 0, 0, 0, 3, 0, 1, 2, 2, 3, 3, 0, 0, 1, 1)
CHUNKS = 3 * YS + 1


def host_of(section):
    place = section * 0
    for layer in range(LAYERS):
        if HOST[layer]:
            place = jnp.where(section == layer, HOST[layer], place)
    return place


def kernel(
    t_ref, latent, mod, wq, wo, stale,
    hid_out, kv_out,
    wbuf, wobuf, modbuf, vecs, cache, hb, hwide, att, own, wide, hst, hland, kvland, nrm,
    wot, base, shifted,
    ld_sem, h_send, h_recv, a_send, a_recv,
    w_send, w_recv, f_send, f_recv, s_send, s_recv, o_send, o_recv,
):
    sec = lax.axis_index("section")
    me = lax.axis_index("seq")
    cfg = lax.axis_index("cfg")
    zh = me // YS
    y = lax.rem(me, YS)
    place = host_of(sec)
    spread = sec < FIRST
    hosting = (sec >= FIRST) & (zh == place)
    helping = (sec >= FIRST) & (zh != place)

    def rows(patch):
        return pl.ds(patch * PATCH_TOK, PATCH_TOK)

    def lanes(number, size=HEAD_DIM):
        return pl.ds(pl.multiple_of(number * size, size), size)

    def remote(src, dst, send, recv, device):
        return pltpu.make_async_remote_copy(
            src_ref=src, dst_ref=dst, send_sem=send, recv_sem=recv,
            device_id=device, device_id_type=MESH,
        )

    def greet(device):
        pl.semaphore_signal(barrier, inc=1, device_id=device, device_id_type=MESH)

    def loop(low, high, act):
        def one(j, _):
            act(j)
            return 0

        lax.fori_loop(low, high, one, 0)

    def each_peer(act, with_self):
        for dz in (2, 1, 3, 0):
            loop(
                1 if dz == 0 and not with_self else 0,
                YS,
                lambda j, dz=dz: act(lax.rem(zh + dz, ZS) * YS + lax.rem(y + j, YS)),
            )

    def each_ring(act, with_self):
        for dy in (2, 1, 3, 0) if with_self else (2, 1, 3):
            act(lax.rem(y + dy, YS))

    def each_helper(act):
        loop(1, ZS, lambda j: act(lax.rem(place + j, ZS)))

    loads = [
        pltpu.make_async_copy(mod, modbuf, ld_sem.at[0]),
        pltpu.make_async_copy(stale, cache.at[zh], ld_sem.at[1]),
        pltpu.make_async_copy(latent, own, ld_sem.at[2]),
        pltpu.make_async_copy(
            wo, wobuf.at[pl.ds(pl.multiple_of(zh * WIDTH, WIDTH), WIDTH)], ld_sem.at[3]
        ),
    ]
    for part in range(3):
        for col in range(YS):
            loads.append(
                pltpu.make_async_copy(
                    wq.at[part, :, col],
                    wbuf.at[col, :, :, lanes(part * ZS + zh)],
                    ld_sem.at[4 + part * YS + col],
                )
            )

    @pl.when(jnp.logical_not(helping))
    def _():
        for one in loads:
            one.start()

    barrier = pltpu.get_barrier_semaphore()

    @pl.when(spread)
    def _():
        each_peer(lambda to: greet((sec, to, cfg)), False)

        @pl.when(sec > 0)
        def _():
            loop(0, SEQ, lambda j: greet((sec - 1, j, cfg)))

    @pl.when(hosting)
    def _():
        each_helper(lambda z: greet((sec, z * YS + y, cfg)))
        greet((sec, me, 1 - cfg))
        each_ring(lambda col: greet((sec, place * YS + col, cfg)), False)

        @pl.when(sec == FIRST)
        def _():
            loop(0, SEQ, lambda j: greet((sec - 1, j, cfg)))

        @pl.when(sec > FIRST)
        def _():
            before = host_of(sec - 1) * YS
            loop(0, YS, lambda j: greet((sec - 1, before + j, cfg)))

    @pl.when(helping)
    def _():
        greet((sec, place * YS + y, cfg))
        pl.semaphore_wait(barrier, 1)

    @pl.when(sec < FIRST - 1)
    def _():
        pl.semaphore_wait(barrier, SEQ - 1 + SEQ)

    @pl.when(sec == FIRST - 1)
    def _():
        pl.semaphore_wait(barrier, SEQ - 1 + YS)

    @pl.when(hosting & (sec < LAYERS - 1))
    def _():
        pl.semaphore_wait(barrier, 2 * YS - 1 + ZS)

    @pl.when(hosting & (sec == LAYERS - 1))
    def _():
        pl.semaphore_wait(barrier, YS - 1 + ZS)

    def chunk_at(number, half, z):
        if number == CHUNKS - 1:
            return wobuf.at[
                pl.ds(pl.multiple_of(z * WIDTH, WIDTH), WIDTH), lanes(half, INNER // 2)
            ]
        part, col = divmod(number, YS)
        return wbuf.at[col, pl.ds(half * 2, 2), :, lanes(part * ZS + z)]

    def chunk_from(number, half):
        if number == CHUNKS - 1:
            return wo.at[:, lanes(half, INNER // 2)]
        part, col = divmod(number, YS)
        return wq.at[part, pl.ds(half * 2, 2), col]

    def w_copy(number):
        return remote(
            chunk_from(number, cfg), chunk_at(number, cfg, zh),
            w_send.at[number], w_recv.at[zh, number], (sec, place * YS + y, cfg),
        )

    def w_landing(number, z):
        spot = chunk_at(number, cfg, z)
        return remote(
            spot, spot, w_send.at[number], w_recv.at[z, number], (sec, z * YS + y, cfg)
        )

    def swap(number, z, half):
        spot = chunk_at(number, half, z)
        return remote(
            spot, spot, f_send.at[z, number], f_recv.at[z, number], (sec, me, 1 - cfg)
        )

    def s_copy():
        return remote(
            stale, cache.at[zh], s_send, s_recv.at[zh], (sec, place * YS + y, cfg)
        )

    def s_landing(z):
        return remote(
            stale, cache.at[z], s_send, s_recv.at[z], (sec, z * YS + y, cfg)
        )

    def o_copy(z, number):
        src = cache.at[z] if number == 2 else hst.at[z, rows(number)]
        dst = kvland if number == 2 else hland.at[rows(number)]
        return remote(src, dst, o_send.at[z, number], o_recv.at[number], (sec, z * YS + y, cfg))

    @pl.when(helping)
    def _():
        s_copy().start()
        for number in range(CHUNKS):
            w_copy(number).start()
        for number in range(CHUNKS):
            w_copy(number).wait_send()
        s_copy().wait_send()
        for number in range(3):
            o_copy(zh, number).wait_recv()
        hid_out[...] = hland[...]
        kv_out[...] = kvland[...]

    def h_copy(patch, section, to):
        return remote(
            own.at[rows(patch)], hb.at[patch, me],
            h_send.at[patch, to], h_recv.at[patch, me], (section, to, cfg),
        )

    def h_landing(patch, source):
        return remote(
            own.at[rows(patch)], hb.at[patch, source],
            h_send.at[patch, source], h_recv.at[patch, source], (sec, source, cfg),
        )

    def wide_copy(patch, to, col):
        return remote(
            wide.at[patch], hwide.at[patch, y],
            h_send.at[patch, col], h_recv.at[patch, y], (sec + 1, to * YS + col, cfg),
        )

    def wide_landing(patch, col):
        return remote(
            wide.at[patch], hwide.at[patch, col],
            h_send.at[patch, col], h_recv.at[patch, col], (sec, col, cfg),
        )

    def a_copy(patch, source, to):
        spot = att.at[patch, source // YS, :, lanes(lax.rem(source, YS))]
        return remote(
            spot, spot, a_send.at[patch, to], a_recv.at[patch, source], (sec, to, cfg)
        )

    def ring_copy(patch, source, to):
        spot = att.at[patch, :, :, lanes(source)]
        return remote(
            spot, spot, a_send.at[patch, to], a_recv.at[patch, source],
            (sec, place * YS + to, cfg),
        )

    def rms(values):
        square = jnp.mean(values * values, axis=-1, keepdims=True)
        return (values * (1.0 / jnp.sqrt(square + EPS_NORM))).astype(jnp.bfloat16)

    def modulation_rows():
        loads[0].wait()
        pick = lax.broadcasted_iota(jnp.int32, (8, D), 0) == t_ref[0]
        for part in range(3):
            row = jnp.sum(
                jnp.where(pick, modbuf[part].astype(jnp.float32), 0.0), axis=0, keepdims=True
            )
            row = jnp.concatenate(
                [
                    row[:, (z * YS + col) * WIDTH : (z * YS + col + 1) * WIDTH]
                    for col in range(YS)
                    for z in range(ZS)
                ],
                axis=1,
            )
            vecs[part] = row + 1.0 if part == 1 else row

    def assemble(patch):
        for col in range(YS):
            hwide[patch, col] = jnp.concatenate(
                [hb[patch, z * YS + col].astype(jnp.float32) for z in range(ZS)], axis=1
            ).astype(jnp.bfloat16)

    def normalise(patch):
        whole = jnp.concatenate(
            [hwide[patch, col].astype(jnp.float32) for col in range(YS)], axis=1
        )
        centred = whole - jnp.mean(whole, axis=-1, keepdims=True)
        spread_of = jnp.mean(centred * centred, axis=-1, keepdims=True)
        nrm[...] = (
            centred * (1.0 / jnp.sqrt(spread_of + EPS_NORM)) * vecs[1] + vecs[0]
        ).astype(jnp.bfloat16)

    def attend(patch, heads):
        for z, _, key, value in heads:
            cache[z, 0, rows(patch), :] = rms(key)
            cache[z, 1, rows(patch), :] = value.astype(jnp.bfloat16)
        queries = [rms(head[1]) for head in heads]
        scores = [
            lax.dot_general(
                query, cache[head[0], 0], (((1,), (1,)), ((), ())),
                preferred_element_type=jnp.float32,
            )
            for head, query in zip(heads, queries)
        ]
        exponents = [jnp.exp(score * HEAD_DIM ** (-0.5)) for score in scores]
        sums = [1.0 / jnp.sum(exponent, axis=-1, keepdims=True) for exponent in exponents]
        probs = [(top * below).astype(jnp.bfloat16) for top, below in zip(exponents, sums)]
        attended = [
            jnp.dot(prob, cache[head[0], 1], preferred_element_type=jnp.float32)
            for head, prob in zip(heads, probs)
        ]
        return [block.astype(jnp.bfloat16) for block in attended]

    def project_out(patch, weight):
        update = None
        for z in range(ZS):
            term = lax.dot_general(
                att[patch, z], weight(z), (((1,), (1,)), ((), ())),
                preferred_element_type=jnp.float32,
            )
            update = term if update is None else update + term
        return update

    @pl.when(spread)
    def _():
        modulation_rows()
        loads[1].wait()
        loads[2].wait()

        @pl.when(sec == 0)
        def _():
            for patch in range(PATCHES):
                each_peer(lambda to: h_copy(patch, sec, to).start(), False)
                hb[patch, me] = own[rows(patch)]

        def front(patch):
            @pl.when(sec == 0)
            def _():
                each_peer(lambda to: h_landing(patch, to).wait_recv(), False)
                each_peer(lambda to: h_copy(patch, sec, to).wait_send(), False)

            @pl.when(sec > 0)
            def _():
                each_peer(lambda to: h_landing(patch, to).wait_recv(), True)

            assemble(patch)
            normalise(patch)
            if patch == 0:
                for one in loads[4:]:
                    one.wait()
            projected = [
                jnp.dot(
                    nrm[...],
                    wbuf[:, :, :, lanes(part * ZS + zh)].reshape(D, HEAD_DIM),
                    preferred_element_type=jnp.float32,
                )
                for part in range(3)
            ]
            att[patch, zh, :, lanes(y)] = attend(patch, [(zh, *projected)])[0]
            each_peer(lambda to: a_copy(patch, me, to).start(), False)

        def back(patch):
            if patch == 0:
                loads[3].wait()
            mine = vecs[2, :, lanes(y, WIDE)]
            gate = jnp.zeros((1, WIDTH), jnp.float32)
            for z in range(ZS):
                gate = gate + jnp.where(zh == z, mine[:, z * WIDTH : (z + 1) * WIDTH], 0.0)
            each_peer(lambda to: a_copy(patch, to, to).wait_recv(), False)
            part = pl.ds(pl.multiple_of(zh * WIDTH, WIDTH), WIDTH)
            update = project_out(patch, lambda z: wobuf[part, z * GROUP : (z + 1) * GROUP])
            result = (hb[patch, me].astype(jnp.float32) + gate * update).astype(jnp.bfloat16)
            own[rows(patch)] = result

            @pl.when(sec < FIRST - 1)
            def _():
                each_peer(lambda to: h_copy(patch, sec + 1, to).start(), True)

            @pl.when(sec == FIRST - 1)
            def _():
                each_ring(
                    lambda col: h_copy(patch, sec + 1, HOST[FIRST] * YS + col).start(), True
                )

            hid_out[rows(patch), :] = result

        for patch in range(PATCHES):
            front(patch)
        for patch in range(PATCHES):
            back(patch)
        kv_out[...] = cache[zh]
        for patch in range(PATCHES):
            each_peer(lambda to: a_copy(patch, me, to).wait_send(), False)

            @pl.when(sec < FIRST - 1)
            def _():
                each_peer(lambda to: h_copy(patch, sec + 1, to).wait_send(), True)

            @pl.when(sec == FIRST - 1)
            def _():
                each_ring(
                    lambda col: h_copy(patch, sec + 1, HOST[FIRST] * YS + col).wait_send(), True
                )

    @pl.when(hosting)
    def _():
        modulation_rows()
        for one in loads[1:]:
            one.wait()
        for number in range(CHUNKS):
            def relay(z, number=number):
                w_landing(number, z).wait_recv()
                swap(number, z, cfg).start()

            each_helper(relay)
        each_helper(lambda z: s_landing(z).wait_recv())
        for number in range(CHUNKS):
            each_helper(lambda z: swap(number, z, 1 - cfg).wait_recv())
            each_helper(lambda z: swap(number, z, cfg).wait_send())
        after = host_of(sec + 1)

        def turn(j):
            at = lanes(j)
            wot[at, :] = wobuf[:, at].T

        loop(0, INNER // HEAD_DIM, turn)

        which = lax.broadcasted_iota(jnp.int32, (16, WIDE), 0)
        shift_sum = None
        for col in range(YS):
            here = slice(col * WIDE, (col + 1) * WIDE)
            scale = vecs[1, :, here]
            high = scale.astype(jnp.bfloat16).astype(jnp.float32)
            stack = jnp.where(
                which == 0, high,
                jnp.where(which == 1, scale - high, jnp.where(which == 2, vecs[0, :, here], 0.0)),
            )
            sums = jnp.dot(
                stack.astype(jnp.bfloat16), wbuf[col].reshape(WIDE, 3 * GROUP),
                preferred_element_type=jnp.float32,
            )
            base[col] = sums[0:1] + sums[1:2]
            shift_sum = sums[2:3] if shift_sum is None else shift_sum + sums[2:3]
        shifted[...] = shift_sum

        def front(patch):
            @pl.when(sec == FIRST)
            def _():
                loop(0, SEQ, lambda j: h_landing(patch, j).wait_recv())
                assemble(patch)

            total, parts = None, []
            for dy in (0, 1, 3, 2):
                col = lax.rem(y + dy, YS)

                @pl.when(sec > FIRST)
                def _(col=col):
                    wide_landing(patch, col).wait_recv()

                block = hwide[patch, col].astype(jnp.float32)
                middle = jnp.mean(block, axis=-1, keepdims=True)
                block = block - middle
                parts.append((col, middle, jnp.sum(block * block, axis=-1, keepdims=True)))
                term = jnp.dot(
                    (block * vecs[1, :, lanes(col, WIDE)]).astype(jnp.bfloat16),
                    wbuf[col].reshape(WIDE, 3 * GROUP),
                    preferred_element_type=jnp.float32,
                )
                total = term if total is None else total + term
            mean = sum(part[1] for part in parts) * (1.0 / YS)
            spread_of = sum(part[2] + WIDE * (part[1] - mean) ** 2 for part in parts) * (1.0 / D)
            for col, middle, _ in parts:
                total = total + (middle - mean) * base[col]
            projected = total * (1.0 / jnp.sqrt(spread_of + EPS_NORM)) + shifted[...]
            attended = attend(
                patch,
                [
                    (z, *[
                        projected[:, part * GROUP + z * HEAD_DIM : part * GROUP + (z + 1) * HEAD_DIM]
                        for part in range(3)
                    ])
                    for z in range(ZS)
                ],
            )
            for z in range(ZS):
                att[patch, z, :, lanes(y)] = attended[z]
            each_ring(lambda col: ring_copy(patch, y, col).start(), False)

        def back(patch):
            each_ring(lambda col: ring_copy(patch, col, col).wait_recv(), False)
            update = None
            for z in range(ZS):
                term = jnp.dot(
                    att[patch, z], wot[z * GROUP : (z + 1) * GROUP],
                    preferred_element_type=jnp.float32,
                )
                update = term if update is None else update + term
            result = hwide[patch, y].astype(jnp.float32) + vecs[2, :, lanes(y, WIDE)] * update
            wide[patch] = result.astype(jnp.bfloat16)

            @pl.when(sec < LAYERS - 1)
            def _():
                each_ring(lambda col: wide_copy(patch, after, col).start(), True)

            for z in range(ZS):
                hst[z, rows(patch)] = result[:, z * WIDTH : (z + 1) * WIDTH].astype(jnp.bfloat16)
            each_helper(lambda z: o_copy(z, patch).start())

        for patch in range(PATCHES):
            front(patch)
        each_helper(lambda z: o_copy(z, 2).start())
        for patch in range(PATCHES):
            back(patch)
        kv_out[...] = cache[place]
        hid_out[...] = hst[place]
        for patch in range(PATCHES):
            each_ring(lambda col: ring_copy(patch, y, col).wait_send(), False)

            @pl.when(sec < LAYERS - 1)
            def _():
                each_ring(lambda col: wide_copy(patch, after, col).wait_send(), True)

        for number in range(3):
            each_helper(lambda z: o_copy(z, number).wait_send())


def on_device(latent, timestep, modulation, qkv_weight, out_weight, stale_kv):
    any_space = pl.BlockSpec(memory_space=pl.ANY)
    in_vmem = pl.BlockSpec(memory_space=pltpu.VMEM)
    bf16 = jnp.bfloat16
    dma = pltpu.SemaphoreType.DMA
    hidden, caches = pl.pallas_call(
        kernel,
        out_shape=(
            jax.ShapeDtypeStruct((TOKENS, WIDTH), bf16),
            jax.ShapeDtypeStruct((2, TOKENS, HEAD_DIM), bf16),
        ),
        in_specs=[pl.BlockSpec(memory_space=pltpu.SMEM)] + [any_space] * 5,
        out_specs=(in_vmem, in_vmem),
        scratch_shapes=[
            pltpu.VMEM((YS, ZS, WIDTH, 3 * GROUP), bf16),
            pltpu.VMEM((WIDE, INNER), bf16),
            pltpu.VMEM((3, 8, D), bf16),
            pltpu.VMEM((3, 1, D), jnp.float32),
            pltpu.VMEM((ZS, 2, TOKENS, HEAD_DIM), bf16),
            pltpu.VMEM((PATCHES, SEQ, PATCH_TOK, WIDTH), bf16),
            pltpu.VMEM((PATCHES, YS, PATCH_TOK, WIDE), bf16),
            pltpu.VMEM((PATCHES, ZS, PATCH_TOK, YS * HEAD_DIM), bf16),
            pltpu.VMEM((TOKENS, WIDTH), bf16),
            pltpu.VMEM((PATCHES, PATCH_TOK, WIDE), bf16),
            pltpu.VMEM((ZS, TOKENS, WIDTH), bf16),
            pltpu.VMEM((TOKENS, WIDTH), bf16),
            pltpu.VMEM((2, TOKENS, HEAD_DIM), bf16),
            pltpu.VMEM((PATCH_TOK, D), bf16),
            pltpu.VMEM((INNER, WIDE), bf16),
            pltpu.VMEM((YS, 1, 3 * GROUP), jnp.float32),
            pltpu.VMEM((1, 3 * GROUP), jnp.float32),
            dma((16,)),
            dma((PATCHES, SEQ)),
            dma((PATCHES, SEQ)),
            dma((PATCHES, SEQ)),
            dma((PATCHES, SEQ)),
            dma((CHUNKS,)),
            dma((ZS, CHUNKS)),
            dma((ZS, CHUNKS)),
            dma((ZS, CHUNKS)),
            dma,
            dma((ZS,)),
            dma((ZS, 3)),
            dma((3,)),
        ],
        compiler_params=pltpu.CompilerParams(
            collective_id=0, has_side_effects=True, vmem_limit_bytes=60 * 1024 * 1024
        ),
    )(
        timestep,
        latent,
        modulation[0].transpose(1, 0, 2),
        qkv_weight[0].transpose(1, 0, 2).reshape(3, ZS, YS, WIDTH, HEAD_DIM),
        out_weight[0].transpose(1, 0),
        stale_kv[0],
    )
    return hidden[None], caches[None]


def solution(mesh):
    placed = (
        P(None, "seq"),
        P(),
        P("section", "cfg", None, None),
        P("section", None, None, "seq"),
        P("section", None, "seq"),
        P("section", None, "cfg", "seq"),
    )
    return jax.shard_map(
        on_device,
        mesh=mesh,
        in_specs=placed,
        out_specs=(P("section", "cfg", "seq"), P("section", None, "cfg", "seq")),
        check_vma=False,
    )
```

```python
import jax
import jax.numpy as jnp
from jax import lax
from jax.experimental import pallas as pl
from jax.experimental.pallas import tpu as pltpu
from jax.sharding import PartitionSpec as P

D = 3072
HEAD_DIM = 128
INNER = 2048
PATCHES = 2
PATCH_TOK = 32
TOKENS = 64
WIDTH = 192
ZS = 4
YS = 4
SEQ = 16
LAYERS = 16
GROUP = ZS * HEAD_DIM
WIDE = ZS * WIDTH
EPS_NORM = 1e-06
MESH = pl.DeviceIdType.MESH

FIRST = 5
HOST = (0, 0, 0, 0, 0, 3, 0, 1, 2, 2, 3, 3, 0, 0, 1, 1)
CHUNKS = 3 * YS + 1
CROSS = 9


def host_of(section):
    place = section * 0
    for layer in range(LAYERS):
        if HOST[layer]:
            place = jnp.where(section == layer, HOST[layer], place)
    return place


def kernel(
    t_ref, latent, mod, wq, wo, stale,
    hid_out, kv_out,
    wbuf, wobuf, modbuf, vecs, cache, hb, hwide, att, own, wide, hst, hland, kvland, nrm,
    wot, base, shifted,
    ld_sem, h_send, h_recv, a_send, a_recv,
    w_send, w_recv, f_send, f_recv, m_send, m_recv, s_send, s_recv, o_send, o_recv,
):
    sec = lax.axis_index("section")
    me = lax.axis_index("seq")
    cfg = lax.axis_index("cfg")
    zh = me // YS
    y = lax.rem(me, YS)
    place = host_of(sec)
    spread = sec < FIRST
    hosting = (sec >= FIRST) & (zh == place)
    helping = (sec >= FIRST) & (zh != place)
    other = 1 - cfg
    crossed = sec >= CROSS
    branch = jnp.where(crossed, other, cfg)

    def core_at(section):
        return jnp.where(section >= CROSS, 1 - branch, branch)


    def rows(patch):
        return pl.ds(patch * PATCH_TOK, PATCH_TOK)

    def lanes(number, size=HEAD_DIM):
        return pl.ds(pl.multiple_of(number * size, size), size)

    def remote(src, dst, send, recv, device):
        return pltpu.make_async_remote_copy(
            src_ref=src, dst_ref=dst, send_sem=send, recv_sem=recv,
            device_id=device, device_id_type=MESH,
        )

    def greet(device):
        pl.semaphore_signal(barrier, inc=1, device_id=device, device_id_type=MESH)

    def loop(low, high, act):
        def one(j, _):
            act(j)
            return 0

        lax.fori_loop(low, high, one, 0)

    def each_peer(act, with_self):
        for dz in (2, 1, 3, 0):
            loop(
                1 if dz == 0 and not with_self else 0,
                YS,
                lambda j, dz=dz: act(lax.rem(zh + dz, ZS) * YS + lax.rem(y + j, YS)),
            )

    def each_ring(act, with_self):
        for dy in (2, 1, 3, 0) if with_self else (2, 1, 3):
            act(lax.rem(y + dy, YS))

    def each_helper(act):
        loop(1, ZS, lambda j: act(lax.rem(place + j, ZS)))

    loads = [
        pltpu.make_async_copy(mod, modbuf, ld_sem.at[0]),
        pltpu.make_async_copy(stale, cache.at[zh], ld_sem.at[1]),
        pltpu.make_async_copy(latent, own, ld_sem.at[2]),
        pltpu.make_async_copy(
            wo, wobuf.at[pl.ds(pl.multiple_of(zh * WIDTH, WIDTH), WIDTH)], ld_sem.at[3]
        ),
    ]
    for part in range(3):
        for col in range(YS):
            loads.append(
                pltpu.make_async_copy(
                    wq.at[part, :, col],
                    wbuf.at[col, :, :, lanes(part * ZS + zh)],
                    ld_sem.at[4 + part * YS + col],
                )
            )

    @pl.when(jnp.logical_not(helping))
    def _():
        for one in loads[2:]:
            one.start()

        @pl.when(jnp.logical_not(crossed))
        def _():
            for one in loads[:2]:
                one.start()

    barrier = pltpu.get_barrier_semaphore()

    @pl.when(spread)
    def _():
        each_peer(lambda to: greet((sec, to, cfg)), False)

        @pl.when(sec > 0)
        def _():
            loop(0, SEQ, lambda j: greet((sec - 1, j, core_at(sec - 1))))

        greet((sec, me, other))

    @pl.when(hosting)
    def _():
        def helper(z):
            greet((sec, z * YS + y, cfg))
            greet((sec, z * YS + y, other))

        each_helper(helper)
        greet((sec, me, other))
        each_ring(lambda col: greet((sec, place * YS + col, cfg)), False)

        @pl.when(sec == FIRST)
        def _():
            loop(0, SEQ, lambda j: greet((sec - 1, j, core_at(sec - 1))))

        @pl.when(sec > FIRST)
        def _():
            before = host_of(sec - 1) * YS
            loop(0, YS, lambda j: greet((sec - 1, before + j, core_at(sec - 1))))

    @pl.when(helping)
    def _():
        greet((sec, place * YS + y, cfg))
        greet((sec, place * YS + y, other))
        pl.semaphore_wait(barrier, 2)

    @pl.when(sec < FIRST - 1)
    def _():
        pl.semaphore_wait(barrier, SEQ + SEQ)

    @pl.when(sec == FIRST - 1)
    def _():
        pl.semaphore_wait(barrier, SEQ + YS)

    @pl.when(hosting & (sec < LAYERS - 1))
    def _():
        pl.semaphore_wait(barrier, 2 * YS + 2 * (ZS - 1))

    @pl.when(hosting & (sec == LAYERS - 1))
    def _():
        pl.semaphore_wait(barrier, YS + 2 * (ZS - 1))

    def chunk_at(number, half, z):
        if number == CHUNKS - 1:
            return wobuf.at[
                pl.ds(pl.multiple_of(z * WIDTH, WIDTH), WIDTH), lanes(half, INNER // 2)
            ]
        part, col = divmod(number, YS)
        return wbuf.at[col, pl.ds(half * 2, 2), :, lanes(part * ZS + z)]

    def chunk_from(number, half):
        if number == CHUNKS - 1:
            return wo.at[:, lanes(half, INNER // 2)]
        part, col = divmod(number, YS)
        return wq.at[part, pl.ds(half * 2, 2), col]

    def w_copy(number):
        return remote(
            chunk_from(number, cfg), chunk_at(number, cfg, zh),
            w_send.at[number], w_recv.at[zh, number], (sec, place * YS + y, cfg),
        )

    def w_landing(number, z):
        spot = chunk_at(number, cfg, z)
        return remote(
            spot, spot, w_send.at[number], w_recv.at[z, number], (sec, z * YS + y, cfg)
        )

    def swap(number, z, half):
        spot = chunk_at(number, half, z)
        return remote(
            spot, spot, f_send.at[z, number], f_recv.at[z, number], (sec, me, 1 - cfg)
        )

    def m_copy():
        return remote(mod, modbuf, m_send, m_recv, (sec, me, other))

    def s_copy(to, core):
        return remote(
            stale, cache.at[zh], s_send, s_recv.at[zh], (sec, to * YS + y, core)
        )

    def s_landing(z):
        return remote(
            stale, cache.at[z], s_send, s_recv.at[z], (sec, z * YS + y, cfg)
        )

    def o_copy(z, number):
        src = cache.at[z] if number == 2 else hst.at[z, rows(number)]
        dst = kvland if number == 2 else hland.at[rows(number)]
        return remote(
            src, dst, o_send.at[z, number], o_recv.at[number], (sec, z * YS + y, branch)
        )

    def take_back():
        for number in range(3):
            o_copy(zh, number).wait_recv()
        hid_out[...] = hland[...]
        kv_out[...] = kvland[...]

    @pl.when(helping)
    def _():
        s_copy(place, branch).start()
        for number in range(CHUNKS):
            w_copy(number).start()
        for number in range(CHUNKS):
            w_copy(number).wait_send()
        s_copy(place, branch).wait_send()
        take_back()

    @pl.when(jnp.logical_not(helping) & crossed)
    def _():
        m_copy().start()
        s_copy(zh, other).start()

    def own_arrays():
        @pl.when(crossed)
        def _():
            m_copy().wait()
            s_copy(zh, other).wait_send()
            s_landing(zh).wait_recv()

        @pl.when(jnp.logical_not(crossed))
        def _():
            loads[0].wait()
            loads[1].wait()

    def h_copy(patch, section, to):
        return remote(
            own.at[rows(patch)], hb.at[patch, me],
            h_send.at[patch, to], h_recv.at[patch, me],
            (section, to, core_at(section)),
        )

    def h_landing(patch, source):
        return remote(
            own.at[rows(patch)], hb.at[patch, source],
            h_send.at[patch, source], h_recv.at[patch, source], (sec, source, cfg),
        )

    def wide_copy(patch, to, col):
        return remote(
            wide.at[patch], hwide.at[patch, y],
            h_send.at[patch, col], h_recv.at[patch, y], (sec + 1, to * YS + col, core_at(sec + 1)),
        )

    def wide_landing(patch, col):
        return remote(
            wide.at[patch], hwide.at[patch, col],
            h_send.at[patch, col], h_recv.at[patch, col], (sec, col, cfg),
        )

    def a_copy(patch, source, to):
        spot = att.at[patch, source // YS, :, lanes(lax.rem(source, YS))]
        return remote(
            spot, spot, a_send.at[patch, to], a_recv.at[patch, source], (sec, to, cfg)
        )

    def ring_copy(patch, source, to):
        spot = att.at[patch, :, :, lanes(source)]
        return remote(
            spot, spot, a_send.at[patch, to], a_recv.at[patch, source],
            (sec, place * YS + to, cfg),
        )

    def rms(values):
        square = jnp.mean(values * values, axis=-1, keepdims=True)
        return (values * (1.0 / jnp.sqrt(square + EPS_NORM))).astype(jnp.bfloat16)

    def modulation_rows():
        own_arrays()
        pick = lax.broadcasted_iota(jnp.int32, (8, D), 0) == t_ref[0]
        for part in range(3):
            row = jnp.sum(
                jnp.where(pick, modbuf[part].astype(jnp.float32), 0.0), axis=0, keepdims=True
            )
            row = jnp.concatenate(
                [
                    row[:, (z * YS + col) * WIDTH : (z * YS + col + 1) * WIDTH]
                    for col in range(YS)
                    for z in range(ZS)
                ],
                axis=1,
            )
            vecs[part] = row + 1.0 if part == 1 else row

    def assemble(patch):
        for col in range(YS):
            hwide[patch, col] = jnp.concatenate(
                [hb[patch, z * YS + col].astype(jnp.float32) for z in range(ZS)], axis=1
            ).astype(jnp.bfloat16)

    def normalise(patch):
        whole = jnp.concatenate(
            [hwide[patch, col].astype(jnp.float32) for col in range(YS)], axis=1
        )
        centred = whole - jnp.mean(whole, axis=-1, keepdims=True)
        spread_of = jnp.mean(centred * centred, axis=-1, keepdims=True)
        nrm[...] = (
            centred * (1.0 / jnp.sqrt(spread_of + EPS_NORM)) * vecs[1] + vecs[0]
        ).astype(jnp.bfloat16)

    def attend(patch, heads):
        for z, _, key, value in heads:
            cache[z, 0, rows(patch), :] = rms(key)
            cache[z, 1, rows(patch), :] = value.astype(jnp.bfloat16)
        queries = [rms(head[1]) for head in heads]
        scores = [
            lax.dot_general(
                query, cache[head[0], 0], (((1,), (1,)), ((), ())),
                preferred_element_type=jnp.float32,
            )
            for head, query in zip(heads, queries)
        ]
        exponents = [jnp.exp(score * HEAD_DIM ** (-0.5)) for score in scores]
        sums = [1.0 / jnp.sum(exponent, axis=-1, keepdims=True) for exponent in exponents]
        probs = [(top * below).astype(jnp.bfloat16) for top, below in zip(exponents, sums)]
        attended = [
            jnp.dot(prob, cache[head[0], 1], preferred_element_type=jnp.float32)
            for head, prob in zip(heads, probs)
        ]
        return [block.astype(jnp.bfloat16) for block in attended]

    def project_out(patch, weight):
        update = None
        for z in range(ZS):
            term = lax.dot_general(
                att[patch, z], weight(z), (((1,), (1,)), ((), ())),
                preferred_element_type=jnp.float32,
            )
            update = term if update is None else update + term
        return update

    def finish(z):
        @pl.when(crossed)
        def _():
            for number in range(3):
                o_copy(z, number).start()
            take_back()
            for number in range(3):
                o_copy(z, number).wait_send()

        @pl.when(jnp.logical_not(crossed))
        def _():
            hid_out[...] = hst[z]
            kv_out[...] = cache[z]

    @pl.when(spread)
    def _():
        loads[2].wait()

        @pl.when(sec == 0)
        def _():
            for patch in range(PATCHES):
                each_peer(lambda to: h_copy(patch, sec, to).start(), False)
                hb[patch, me] = own[rows(patch)]

        modulation_rows()

        def front(patch):
            @pl.when(sec == 0)
            def _():
                each_peer(lambda to: h_landing(patch, to).wait_recv(), False)
                each_peer(lambda to: h_copy(patch, sec, to).wait_send(), False)

            @pl.when(sec > 0)
            def _():
                each_peer(lambda to: h_landing(patch, to).wait_recv(), True)

            assemble(patch)
            normalise(patch)
            if patch == 0:
                for one in loads[4:]:
                    one.wait()
            projected = [
                jnp.dot(
                    nrm[...],
                    wbuf[:, :, :, lanes(part * ZS + zh)].reshape(D, HEAD_DIM),
                    preferred_element_type=jnp.float32,
                )
                for part in range(3)
            ]
            att[patch, zh, :, lanes(y)] = attend(patch, [(zh, *projected)])[0]
            each_peer(lambda to: a_copy(patch, me, to).start(), False)

        def back(patch):
            if patch == 0:
                loads[3].wait()
            mine = vecs[2, :, lanes(y, WIDE)]
            gate = jnp.zeros((1, WIDTH), jnp.float32)
            for z in range(ZS):
                gate = gate + jnp.where(zh == z, mine[:, z * WIDTH : (z + 1) * WIDTH], 0.0)
            each_peer(lambda to: a_copy(patch, to, to).wait_recv(), False)
            part = pl.ds(pl.multiple_of(zh * WIDTH, WIDTH), WIDTH)
            update = project_out(patch, lambda z: wobuf[part, z * GROUP : (z + 1) * GROUP])
            result = (hb[patch, me].astype(jnp.float32) + gate * update).astype(jnp.bfloat16)
            own[rows(patch)] = result

            @pl.when(sec < FIRST - 1)
            def _():
                each_peer(lambda to: h_copy(patch, sec + 1, to).start(), True)

            @pl.when(sec == FIRST - 1)
            def _():
                each_ring(
                    lambda col: h_copy(patch, sec + 1, HOST[FIRST] * YS + col).start(), True
                )

            hst[zh, rows(patch), :] = result

        for patch in range(PATCHES):
            front(patch)
        for patch in range(PATCHES):
            back(patch)
        finish(zh)
        for patch in range(PATCHES):
            each_peer(lambda to: a_copy(patch, me, to).wait_send(), False)

            @pl.when(sec < FIRST - 1)
            def _():
                each_peer(lambda to: h_copy(patch, sec + 1, to).wait_send(), True)

            @pl.when(sec == FIRST - 1)
            def _():
                each_ring(
                    lambda col: h_copy(patch, sec + 1, HOST[FIRST] * YS + col).wait_send(), True
                )

    @pl.when(hosting)
    def _():
        modulation_rows()
        for one in loads[2:]:
            one.wait()
        for number in range(CHUNKS):
            def relay(z, number=number):
                w_landing(number, z).wait_recv()
                swap(number, z, cfg).start()

            each_helper(relay)
        each_helper(lambda z: s_landing(z).wait_recv())
        for number in range(CHUNKS):
            each_helper(lambda z: swap(number, z, 1 - cfg).wait_recv())
            each_helper(lambda z: swap(number, z, cfg).wait_send())
        after = host_of(sec + 1)

        def turn(j):
            at = lanes(j)
            wot[at, :] = wobuf[:, at].T

        loop(0, INNER // HEAD_DIM, turn)

        which = lax.broadcasted_iota(jnp.int32, (16, WIDE), 0)
        shift_sum = None
        for col in range(YS):
            here = slice(col * WIDE, (col + 1) * WIDE)
            scale = vecs[1, :, here]
            high = scale.astype(jnp.bfloat16).astype(jnp.float32)
            stack = jnp.where(
                which == 0, high,
                jnp.where(which == 1, scale - high, jnp.where(which == 2, vecs[0, :, here], 0.0)),
            )
            sums = jnp.dot(
                stack.astype(jnp.bfloat16), wbuf[col].reshape(WIDE, 3 * GROUP),
                preferred_element_type=jnp.float32,
            )
            base[col] = sums[0:1] + sums[1:2]
            shift_sum = sums[2:3] if shift_sum is None else shift_sum + sums[2:3]
        shifted[...] = shift_sum

        def front(patch):
            @pl.when(sec == FIRST)
            def _():
                loop(0, SEQ, lambda j: h_landing(patch, j).wait_recv())
                assemble(patch)

            total, parts = None, []
            for dy in (2, 3, 1, 0):
                col = lax.rem(y + dy, YS)

                @pl.when(sec > FIRST)
                def _(col=col):
                    wide_landing(patch, col).wait_recv()

                block = hwide[patch, col].astype(jnp.float32)
                middle = jnp.mean(block, axis=-1, keepdims=True)
                block = block - middle
                parts.append((col, middle, jnp.sum(block * block, axis=-1, keepdims=True)))
                term = jnp.dot(
                    (block * vecs[1, :, lanes(col, WIDE)]).astype(jnp.bfloat16),
                    wbuf[col].reshape(WIDE, 3 * GROUP),
                    preferred_element_type=jnp.float32,
                )
                total = term if total is None else total + term
            mean = sum(part[1] for part in parts) * (1.0 / YS)
            spread_of = sum(part[2] + WIDE * (part[1] - mean) ** 2 for part in parts) * (1.0 / D)
            for col, middle, _ in parts:
                total = total + (middle - mean) * base[col]
            projected = total * (1.0 / jnp.sqrt(spread_of + EPS_NORM)) + shifted[...]
            attended = attend(
                patch,
                [
                    (z, *[
                        projected[:, part * GROUP + z * HEAD_DIM : part * GROUP + (z + 1) * HEAD_DIM]
                        for part in range(3)
                    ])
                    for z in range(ZS)
                ],
            )
            for z in range(ZS):
                att[patch, z, :, lanes(y)] = attended[z]
            each_ring(lambda col: ring_copy(patch, y, col).start(), False)

        def back(patch):
            each_ring(lambda col: ring_copy(patch, col, col).wait_recv(), False)
            update = None
            for z in range(ZS):
                term = jnp.dot(
                    att[patch, z], wot[z * GROUP : (z + 1) * GROUP],
                    preferred_element_type=jnp.float32,
                )
                update = term if update is None else update + term
            result = hwide[patch, y].astype(jnp.float32) + vecs[2, :, lanes(y, WIDE)] * update
            wide[patch] = result.astype(jnp.bfloat16)

            @pl.when(sec < LAYERS - 1)
            def _():
                each_ring(lambda col: wide_copy(patch, after, col).start(), True)

            for z in range(ZS):
                hst[z, rows(patch)] = result[:, z * WIDTH : (z + 1) * WIDTH].astype(jnp.bfloat16)
            each_helper(lambda z: o_copy(z, patch).start())

        for patch in range(PATCHES):
            front(patch)
        each_helper(lambda z: o_copy(z, 2).start())
        for patch in range(PATCHES):
            back(patch)
        finish(place)
        for patch in range(PATCHES):
            each_ring(lambda col: ring_copy(patch, y, col).wait_send(), False)

            @pl.when(sec < LAYERS - 1)
            def _():
                each_ring(lambda col: wide_copy(patch, after, col).wait_send(), True)

        for number in range(3):
            each_helper(lambda z: o_copy(z, number).wait_send())


def on_device(latent, timestep, modulation, qkv_weight, out_weight, stale_kv):
    any_space = pl.BlockSpec(memory_space=pl.ANY)
    in_vmem = pl.BlockSpec(memory_space=pltpu.VMEM)
    bf16 = jnp.bfloat16
    dma = pltpu.SemaphoreType.DMA
    hidden, caches = pl.pallas_call(
        kernel,
        out_shape=(
            jax.ShapeDtypeStruct((TOKENS, WIDTH), bf16),
            jax.ShapeDtypeStruct((2, TOKENS, HEAD_DIM), bf16),
        ),
        in_specs=[pl.BlockSpec(memory_space=pltpu.SMEM)] + [any_space] * 5,
        out_specs=(in_vmem, in_vmem),
        scratch_shapes=[
            pltpu.VMEM((YS, ZS, WIDTH, 3 * GROUP), bf16),
            pltpu.VMEM((WIDE, INNER), bf16),
            pltpu.VMEM((3, 8, D), bf16),
            pltpu.VMEM((3, 1, D), jnp.float32),
            pltpu.VMEM((ZS, 2, TOKENS, HEAD_DIM), bf16),
            pltpu.VMEM((PATCHES, SEQ, PATCH_TOK, WIDTH), bf16),
            pltpu.VMEM((PATCHES, YS, PATCH_TOK, WIDE), bf16),
            pltpu.VMEM((PATCHES, ZS, PATCH_TOK, YS * HEAD_DIM), bf16),
            pltpu.VMEM((TOKENS, WIDTH), bf16),
            pltpu.VMEM((PATCHES, PATCH_TOK, WIDE), bf16),
            pltpu.VMEM((ZS, TOKENS, WIDTH), bf16),
            pltpu.VMEM((TOKENS, WIDTH), bf16),
            pltpu.VMEM((2, TOKENS, HEAD_DIM), bf16),
            pltpu.VMEM((PATCH_TOK, D), bf16),
            pltpu.VMEM((INNER, WIDE), bf16),
            pltpu.VMEM((YS, 1, 3 * GROUP), jnp.float32),
            pltpu.VMEM((1, 3 * GROUP), jnp.float32),
            dma((16,)),
            dma((PATCHES, SEQ)),
            dma((PATCHES, SEQ)),
            dma((PATCHES, SEQ)),
            dma((PATCHES, SEQ)),
            dma((CHUNKS,)),
            dma((ZS, CHUNKS)),
            dma((ZS, CHUNKS)),
            dma((ZS, CHUNKS)),
            dma,
            dma,
            dma,
            dma((ZS,)),
            dma((ZS, 3)),
            dma((3,)),
        ],
        compiler_params=pltpu.CompilerParams(
            collective_id=0, has_side_effects=True, vmem_limit_bytes=60 * 1024 * 1024
        ),
    )(
        timestep,
        latent,
        modulation[0].transpose(1, 0, 2),
        qkv_weight[0].transpose(1, 0, 2).reshape(3, ZS, YS, WIDTH, HEAD_DIM),
        out_weight[0].transpose(1, 0),
        stale_kv[0],
    )
    return hidden[None], caches[None]


def solution(mesh):
    placed = (
        P(None, "seq"),
        P(),
        P("section", "cfg", None, None),
        P("section", None, None, "seq"),
        P("section", None, "seq"),
        P("section", None, "cfg", "seq"),
    )
    return jax.shard_map(
        on_device,
        mesh=mesh,
        in_specs=placed,
        out_specs=(P("section", "cfg", "seq"), P("section", None, "cfg", "seq")),
        check_vma=False,
    )
```

```python
import jax
import jax.numpy as jnp
from jax import lax
from jax.experimental import pallas as pl
from jax.experimental.pallas import tpu as pltpu
from jax.sharding import PartitionSpec as P

D = 3072
HEAD_DIM = 128
INNER = 2048
PATCHES = 2
PATCH_TOK = 32
TOKENS = 64
WIDTH = 192
ZS = 4
YS = 4
SEQ = 16
LAYERS = 16
GROUP = ZS * HEAD_DIM
WIDE = ZS * WIDTH
EPS_NORM = 1e-06
MESH = pl.DeviceIdType.MESH

FIRST = 5
HOST = (0, 0, 0, 0, 0, 3, 0, 1, 2, 2, 3, 3, 0, 0, 1, 1)
CHUNKS = 3 * YS + 1
CROSS = 10


def host_of(section):
    place = section * 0
    for layer in range(LAYERS):
        if HOST[layer]:
            place = jnp.where(section == layer, HOST[layer], place)
    return place


def kernel(
    t_ref, latent, mod, wq, wo, stale,
    hid_out, kv_out,
    wbuf, wobuf, modbuf, vecs, cache, hb, hwide, att, own, wide, hst, hland, kvland,
    wot, base, shifted,
    ld_sem, h_send, h_recv, a_send, a_recv,
    w_send, w_recv, f_send, f_recv, m_send, m_recv, s_send, s_recv, o_send, o_recv,
):
    sec = lax.axis_index("section")
    me = lax.axis_index("seq")
    cfg = lax.axis_index("cfg")
    zh = me // YS
    y = lax.rem(me, YS)
    place = host_of(sec)
    spread = sec < FIRST
    hosting = (sec >= FIRST) & (zh == place)
    helping = (sec >= FIRST) & (zh != place)
    other = 1 - cfg
    crossed = sec >= CROSS
    branch = jnp.where(crossed, other, cfg)

    def core_at(section):
        return jnp.where(section >= CROSS, 1 - branch, branch)


    def rows(patch):
        return pl.ds(patch * PATCH_TOK, PATCH_TOK)

    def lanes(number, size=HEAD_DIM):
        return pl.ds(pl.multiple_of(number * size, size), size)

    def remote(src, dst, send, recv, device):
        return pltpu.make_async_remote_copy(
            src_ref=src, dst_ref=dst, send_sem=send, recv_sem=recv,
            device_id=device, device_id_type=MESH,
        )

    def greet(device):
        pl.semaphore_signal(barrier, inc=1, device_id=device, device_id_type=MESH)

    def loop(low, high, act):
        def one(j, _):
            act(j)
            return 0

        lax.fori_loop(low, high, one, 0)

    def each_peer(act, with_self):
        for dz in (2, 1, 3, 0):
            loop(
                1 if dz == 0 and not with_self else 0,
                YS,
                lambda j, dz=dz: act(lax.rem(zh + dz, ZS) * YS + lax.rem(y + j, YS)),
            )

    def each_ring(act, with_self):
        for dy in (2, 1, 3, 0) if with_self else (2, 1, 3):
            act(lax.rem(y + dy, YS))

    def each_helper(act):
        loop(1, ZS, lambda j: act(lax.rem(place + j, ZS)))

    loads = [
        pltpu.make_async_copy(mod, modbuf, ld_sem.at[0]),
        pltpu.make_async_copy(stale, cache.at[zh], ld_sem.at[1]),
        pltpu.make_async_copy(latent, own, ld_sem.at[2]),
        pltpu.make_async_copy(
            wo, wobuf.at[pl.ds(pl.multiple_of(zh * WIDTH, WIDTH), WIDTH)], ld_sem.at[3]
        ),
    ]
    for part in range(3):
        for col in range(YS):
            loads.append(
                pltpu.make_async_copy(
                    wq.at[part, :, col],
                    wbuf.at[part * ZS + zh, col],
                    ld_sem.at[4 + part * YS + col],
                )
            )

    @pl.when(jnp.logical_not(helping))
    def _():
        for one in loads[2:]:
            one.start()

        @pl.when(jnp.logical_not(crossed))
        def _():
            for one in loads[:2]:
                one.start()

    barrier = pltpu.get_barrier_semaphore()

    @pl.when(spread)
    def _():
        each_peer(lambda to: greet((sec, to, cfg)), False)

        @pl.when(sec > 0)
        def _():
            loop(0, SEQ, lambda j: greet((sec - 1, j, core_at(sec - 1))))

        greet((sec, me, other))

    @pl.when(hosting)
    def _():
        def helper(z):
            greet((sec, z * YS + y, cfg))
            greet((sec, z * YS + y, other))

        each_helper(helper)
        greet((sec, me, other))
        each_ring(lambda col: greet((sec, place * YS + col, cfg)), False)

        @pl.when(sec == FIRST)
        def _():
            loop(0, SEQ, lambda j: greet((sec - 1, j, core_at(sec - 1))))

        @pl.when(sec > FIRST)
        def _():
            before = host_of(sec - 1) * YS
            loop(0, YS, lambda j: greet((sec - 1, before + j, core_at(sec - 1))))

    @pl.when(helping)
    def _():
        greet((sec, place * YS + y, cfg))
        greet((sec, place * YS + y, other))
        pl.semaphore_wait(barrier, 2)

    @pl.when(sec < FIRST - 1)
    def _():
        pl.semaphore_wait(barrier, SEQ + SEQ)

    @pl.when(sec == FIRST - 1)
    def _():
        pl.semaphore_wait(barrier, SEQ + YS)

    @pl.when(hosting & (sec < LAYERS - 1))
    def _():
        pl.semaphore_wait(barrier, 2 * YS + 2 * (ZS - 1))

    @pl.when(hosting & (sec == LAYERS - 1))
    def _():
        pl.semaphore_wait(barrier, YS + 2 * (ZS - 1))

    def chunk_at(number, half, z):
        if number == CHUNKS - 1:
            return wobuf.at[
                pl.ds(pl.multiple_of(z * WIDTH, WIDTH), WIDTH), lanes(half, INNER // 2)
            ]
        part, col = divmod(number, YS)
        return wbuf.at[part * ZS + z, col, pl.ds(half * 2, 2)]

    def chunk_from(number, half):
        if number == CHUNKS - 1:
            return wo.at[:, lanes(half, INNER // 2)]
        part, col = divmod(number, YS)
        return wq.at[part, pl.ds(half * 2, 2), col]

    def w_copy(number):
        return remote(
            chunk_from(number, cfg), chunk_at(number, cfg, zh),
            w_send.at[number], w_recv.at[zh, number], (sec, place * YS + y, cfg),
        )

    def w_landing(number, z):
        spot = chunk_at(number, cfg, z)
        return remote(
            spot, spot, w_send.at[number], w_recv.at[z, number], (sec, z * YS + y, cfg)
        )

    def swap(number, z, half):
        spot = chunk_at(number, half, z)
        return remote(
            spot, spot, f_send.at[z, number], f_recv.at[z, number], (sec, me, 1 - cfg)
        )

    def m_copy():
        return remote(mod, modbuf, m_send, m_recv, (sec, me, other))

    def s_copy(to, core):
        return remote(
            stale, cache.at[zh], s_send, s_recv.at[zh], (sec, to * YS + y, core)
        )

    def s_landing(z):
        return remote(
            stale, cache.at[z], s_send, s_recv.at[z], (sec, z * YS + y, cfg)
        )

    def o_copy(z, number):
        src = cache.at[z] if number == 2 else hst.at[z, rows(number)]
        dst = kvland if number == 2 else hland.at[rows(number)]
        return remote(
            src, dst, o_send.at[z, number], o_recv.at[number], (sec, z * YS + y, branch)
        )

    def take_back():
        for number in range(3):
            o_copy(zh, number).wait_recv()
        hid_out[...] = hland[...]
        kv_out[...] = kvland[...]

    @pl.when(helping)
    def _():
        s_copy(place, branch).start()
        for number in range(CHUNKS):
            w_copy(number).start()
        for number in range(CHUNKS):
            w_copy(number).wait_send()
        s_copy(place, branch).wait_send()
        take_back()

    @pl.when(jnp.logical_not(helping) & crossed)
    def _():
        m_copy().start()
        s_copy(zh, other).start()

    def own_arrays():
        @pl.when(crossed)
        def _():
            m_copy().wait()
            s_copy(zh, other).wait_send()
            s_landing(zh).wait_recv()

        @pl.when(jnp.logical_not(crossed))
        def _():
            loads[0].wait()
            loads[1].wait()

    def h_copy(patch, section, to):
        return remote(
            own.at[rows(patch)], hb.at[patch, me],
            h_send.at[patch, to], h_recv.at[patch, me],
            (section, to, core_at(section)),
        )

    def h_landing(patch, source):
        return remote(
            own.at[rows(patch)], hb.at[patch, source],
            h_send.at[patch, source], h_recv.at[patch, source], (sec, source, cfg),
        )

    def wide_copy(patch, to, col):
        return remote(
            wide.at[patch], hwide.at[patch, y],
            h_send.at[patch, col], h_recv.at[patch, y], (sec + 1, to * YS + col, core_at(sec + 1)),
        )

    def wide_landing(patch, col):
        return remote(
            wide.at[patch], hwide.at[patch, col],
            h_send.at[patch, col], h_recv.at[patch, col], (sec, col, cfg),
        )

    def a_copy(patch, source, to):
        spot = att.at[patch, source // YS, :, lanes(lax.rem(source, YS))]
        return remote(
            spot, spot, a_send.at[patch, to], a_recv.at[patch, source], (sec, to, cfg)
        )

    def ring_copy(patch, source, to):
        spot = att.at[patch, source]
        return remote(
            spot, spot, a_send.at[patch, to], a_recv.at[patch, source],
            (sec, place * YS + to, cfg),
        )

    def rms(values):
        square = jnp.mean(values * values, axis=-1, keepdims=True)
        return (values * (1.0 / jnp.sqrt(square + EPS_NORM))).astype(jnp.bfloat16)

    def weights(col):
        return jnp.concatenate(
            [wbuf[number, col].reshape(WIDE, HEAD_DIM) for number in range(3 * ZS)], axis=1
        )

    def own_weights(z):
        return jnp.concatenate(
            [wbuf[part * ZS + zh, :, z].reshape(WIDE, HEAD_DIM) for part in range(3)], axis=1
        )

    def column_sums(weights_of):
        which = lax.broadcasted_iota(jnp.int32, (16, WIDE), 0)
        shift_sum = None
        for number in range(YS):
            here = slice(number * WIDE, (number + 1) * WIDE)
            scale = vecs[1, :, here]
            high = scale.astype(jnp.bfloat16).astype(jnp.float32)
            stack = jnp.where(
                which == 0, high,
                jnp.where(which == 1, scale - high, jnp.where(which == 2, vecs[0, :, here], 0.0)),
            )
            sums = jnp.dot(
                stack.astype(jnp.bfloat16), weights_of(number), preferred_element_type=jnp.float32
            )
            size = sums.shape[1]
            base[number, :, :size] = sums[0:1] + sums[1:2]
            shift_sum = sums[2:3] if shift_sum is None else shift_sum + sums[2:3]
        shifted[:, :size] = shift_sum

    def project(order, block_of, weights_of, size):
        total, parts = None, []
        for number in order:
            block = block_of(number)
            middle = jnp.mean(block, axis=-1, keepdims=True)
            block = block - middle
            parts.append((number, middle, jnp.sum(block * block, axis=-1, keepdims=True)))
            term = jnp.dot(
                (block * vecs[1, :, lanes(number, WIDE)]).astype(jnp.bfloat16),
                weights_of(number),
                preferred_element_type=jnp.float32,
            )
            total = term if total is None else total + term
        mean = sum(part[1] for part in parts) * (1.0 / YS)
        spread_of = sum(part[2] + WIDE * (part[1] - mean) ** 2 for part in parts) * (1.0 / D)
        for number, middle, _ in parts:
            total = total + (middle - mean) * base[number, :, :size]
        return total * (1.0 / jnp.sqrt(spread_of + EPS_NORM)) + shifted[:, :size]

    def modulation_rows(ring):
        own_arrays()
        pick = lax.broadcasted_iota(jnp.int32, (8, D), 0) == t_ref[0]
        for part in range(3):
            row = jnp.sum(
                jnp.where(pick, modbuf[part].astype(jnp.float32), 0.0), axis=0, keepdims=True
            )
            if ring:
                row = jnp.concatenate(
                    [
                        row[:, (z * YS + col) * WIDTH : (z * YS + col + 1) * WIDTH]
                        for col in range(YS)
                        for z in range(ZS)
                    ],
                    axis=1,
                )
            vecs[part] = row + 1.0 if part == 1 else row

    def assemble(patch):
        for col in range(YS):
            hwide[patch, col] = jnp.concatenate(
                [hb[patch, z * YS + col].astype(jnp.float32) for z in range(ZS)], axis=1
            ).astype(jnp.bfloat16)

    def attend(patch, heads):
        for z, _, key, value in heads:
            cache[z, 0, rows(patch), :] = rms(key)
            cache[z, 1, rows(patch), :] = value.astype(jnp.bfloat16)
        queries = [rms(head[1]) for head in heads]
        scores = [
            lax.dot_general(
                query, cache[head[0], 0], (((1,), (1,)), ((), ())),
                preferred_element_type=jnp.float32,
            )
            for head, query in zip(heads, queries)
        ]
        exponents = [jnp.exp(score * HEAD_DIM ** (-0.5)) for score in scores]
        sums = [1.0 / jnp.sum(exponent, axis=-1, keepdims=True) for exponent in exponents]
        probs = [(top * below).astype(jnp.bfloat16) for top, below in zip(exponents, sums)]
        attended = [
            jnp.dot(prob, cache[head[0], 1], preferred_element_type=jnp.float32)
            for head, prob in zip(heads, probs)
        ]
        return [block.astype(jnp.bfloat16) for block in attended]

    def finish(z):
        @pl.when(crossed)
        def _():
            for number in range(3):
                o_copy(z, number).start()
            take_back()
            for number in range(3):
                o_copy(z, number).wait_send()

        @pl.when(jnp.logical_not(crossed))
        def _():
            hid_out[...] = hst[z]
            kv_out[...] = cache[z]

    @pl.when(spread)
    def _():
        loads[2].wait()

        @pl.when(sec == 0)
        def _():
            for patch in range(PATCHES):
                each_peer(lambda to: h_copy(patch, sec, to).start(), False)
                hb[patch, me] = own[rows(patch)]

        modulation_rows(False)
        for one in loads[4:]:
            one.wait()
        column_sums(own_weights)

        def front(patch):
            def block_of(z):
                def arrived(col):
                    @pl.when((sec > 0) | (z * YS + col != me))
                    def _():
                        h_landing(patch, z * YS + col).wait_recv()

                loop(0, YS, arrived)
                return jnp.concatenate(
                    [hb[patch, z * YS + col].astype(jnp.float32) for col in range(YS)], axis=1
                )

            projected = project(
                [lax.rem(zh + dz, ZS) for dz in (0, 1, 3, 2)], block_of, own_weights, 3 * HEAD_DIM
            )
            three = [projected[:, part * HEAD_DIM : (part + 1) * HEAD_DIM] for part in range(3)]
            att[patch, zh, :, lanes(y)] = attend(patch, [(zh, *three)])[0]
            each_peer(lambda to: a_copy(patch, me, to).start(), False)

            @pl.when(sec == 0)
            def _():
                each_peer(lambda to: h_copy(patch, sec, to).wait_send(), False)

        def back(patch):
            if patch == 0:
                loads[3].wait()
            mine = vecs[2, :, lanes(zh, WIDE)]
            gate = jnp.zeros((1, WIDTH), jnp.float32)
            for col in range(YS):
                gate = gate + jnp.where(y == col, mine[:, col * WIDTH : (col + 1) * WIDTH], 0.0)
            part = pl.ds(pl.multiple_of(zh * WIDTH, WIDTH), WIDTH)
            update = None
            for dz in (0, 1, 3, 2):
                z = lax.rem(zh + dz, ZS)
                loop(
                    0 if dz else 1,
                    YS,
                    lambda j, z=z: a_copy(
                        patch, z * YS + lax.rem(y + j, YS), z * YS + lax.rem(y + j, YS)
                    ).wait_recv(),
                )
                term = lax.dot_general(
                    att[patch, z], wobuf[part, lanes(z, GROUP)],
                    (((1,), (1,)), ((), ())),
                    preferred_element_type=jnp.float32,
                )
                update = term if update is None else update + term
            result = (hb[patch, me].astype(jnp.float32) + gate * update).astype(jnp.bfloat16)
            own[rows(patch)] = result

            @pl.when(sec < FIRST - 1)
            def _():
                each_peer(lambda to: h_copy(patch, sec + 1, to).start(), True)

            @pl.when(sec == FIRST - 1)
            def _():
                each_ring(
                    lambda col: h_copy(patch, sec + 1, HOST[FIRST] * YS + col).start(), True
                )

            hst[zh, rows(patch), :] = result

        for patch in range(PATCHES):
            front(patch)
        for patch in range(PATCHES):
            back(patch)
        finish(zh)
        for patch in range(PATCHES):
            each_peer(lambda to: a_copy(patch, me, to).wait_send(), False)

            @pl.when(sec < FIRST - 1)
            def _():
                each_peer(lambda to: h_copy(patch, sec + 1, to).wait_send(), True)

            @pl.when(sec == FIRST - 1)
            def _():
                each_ring(
                    lambda col: h_copy(patch, sec + 1, HOST[FIRST] * YS + col).wait_send(), True
                )

    @pl.when(hosting)
    def _():
        modulation_rows(True)
        for one in loads[2:]:
            one.wait()
        for number in range(CHUNKS):
            def relay(z, number=number):
                w_landing(number, z).wait_recv()
                swap(number, z, cfg).start()

            each_helper(relay)
        each_helper(lambda z: s_landing(z).wait_recv())
        for number in range(CHUNKS):
            each_helper(lambda z: swap(number, z, 1 - cfg).wait_recv())
            each_helper(lambda z: swap(number, z, cfg).wait_send())
        after = host_of(sec + 1)

        def turn(j):
            at = lanes(j)
            wot[lanes(lax.rem(j, YS) * ZS + j // YS), :] = wobuf[:, at].T

        loop(0, INNER // HEAD_DIM, turn)

        column_sums(weights)

        def front(patch):
            @pl.when(sec == FIRST)
            def _():
                loop(0, SEQ, lambda j: h_landing(patch, j).wait_recv())
                assemble(patch)

            def block_of(col):
                @pl.when(sec > FIRST)
                def _():
                    wide_landing(patch, col).wait_recv()

                return hwide[patch, col].astype(jnp.float32)

            projected = project(
                [lax.rem(y + dy, YS) for dy in (2, 3, 1, 0)], block_of, weights, 3 * GROUP
            )
            attended = attend(
                patch,
                [
                    (z, *[
                        projected[:, part * GROUP + z * HEAD_DIM : part * GROUP + (z + 1) * HEAD_DIM]
                        for part in range(3)
                    ])
                    for z in range(ZS)
                ],
            )
            att[patch, y] = jnp.concatenate(attended, axis=1)
            each_ring(lambda col: ring_copy(patch, y, col).start(), False)

        def back(patch):
            update = None
            for dy in (0, 3, 1, 2):
                col = lax.rem(y + dy, YS)
                if dy:
                    ring_copy(patch, col, col).wait_recv()
                term = jnp.dot(
                    att[patch, col], wot[lanes(col, GROUP), :],
                    preferred_element_type=jnp.float32,
                )
                update = term if update is None else update + term
            result = hwide[patch, y].astype(jnp.float32) + vecs[2, :, lanes(y, WIDE)] * update
            wide[patch] = result.astype(jnp.bfloat16)

            @pl.when(sec < LAYERS - 1)
            def _():
                each_ring(lambda col: wide_copy(patch, after, col).start(), True)

            for z in range(ZS):
                hst[z, rows(patch)] = result[:, z * WIDTH : (z + 1) * WIDTH].astype(jnp.bfloat16)

            @pl.when(sec == LAYERS - 1)
            def _():
                each_helper(lambda z: o_copy(z, patch).start())

        for patch in range(PATCHES):
            front(patch)

        @pl.when(sec == LAYERS - 1)
        def _():
            each_helper(lambda z: o_copy(z, 2).start())

        for patch in range(PATCHES):
            back(patch)
        for patch in range(PATCHES):
            each_ring(lambda col: ring_copy(patch, y, col).wait_send(), False)

            @pl.when(sec < LAYERS - 1)
            def _():
                each_ring(lambda col: wide_copy(patch, after, col).wait_send(), True)

        @pl.when(sec < LAYERS - 1)
        def _():
            for number in range(3):
                each_helper(lambda z: o_copy(z, number).start())

        for number in range(3):
            each_helper(lambda z: o_copy(z, number).wait_send())
        finish(place)


def on_device(latent, timestep, modulation, qkv_weight, out_weight, stale_kv):
    any_space = pl.BlockSpec(memory_space=pl.ANY)
    in_vmem = pl.BlockSpec(memory_space=pltpu.VMEM)
    bf16 = jnp.bfloat16
    dma = pltpu.SemaphoreType.DMA
    hidden, caches = pl.pallas_call(
        kernel,
        out_shape=(
            jax.ShapeDtypeStruct((TOKENS, WIDTH), bf16),
            jax.ShapeDtypeStruct((2, TOKENS, HEAD_DIM), bf16),
        ),
        in_specs=[pl.BlockSpec(memory_space=pltpu.SMEM)] + [any_space] * 5,
        out_specs=(in_vmem, in_vmem),
        scratch_shapes=[
            pltpu.VMEM((3 * ZS, YS, ZS, WIDTH, HEAD_DIM), bf16),
            pltpu.VMEM((WIDE, INNER), bf16),
            pltpu.VMEM((3, 8, D), bf16),
            pltpu.VMEM((3, 1, D), jnp.float32),
            pltpu.VMEM((ZS, 2, TOKENS, HEAD_DIM), bf16),
            pltpu.VMEM((PATCHES, SEQ, PATCH_TOK, WIDTH), bf16),
            pltpu.VMEM((PATCHES, YS, PATCH_TOK, WIDE), bf16),
            pltpu.VMEM((PATCHES, ZS, PATCH_TOK, YS * HEAD_DIM), bf16),
            pltpu.VMEM((TOKENS, WIDTH), bf16),
            pltpu.VMEM((PATCHES, PATCH_TOK, WIDE), bf16),
            pltpu.VMEM((ZS, TOKENS, WIDTH), bf16),
            pltpu.VMEM((TOKENS, WIDTH), bf16),
            pltpu.VMEM((2, TOKENS, HEAD_DIM), bf16),
            pltpu.VMEM((INNER, WIDE), bf16),
            pltpu.VMEM((YS, 1, 3 * GROUP), jnp.float32),
            pltpu.VMEM((1, 3 * GROUP), jnp.float32),
            dma((16,)),
            dma((PATCHES, SEQ)),
            dma((PATCHES, SEQ)),
            dma((PATCHES, SEQ)),
            dma((PATCHES, SEQ)),
            dma((CHUNKS,)),
            dma((ZS, CHUNKS)),
            dma((ZS, CHUNKS)),
            dma((ZS, CHUNKS)),
            dma,
            dma,
            dma,
            dma((ZS,)),
            dma((ZS, 3)),
            dma((3,)),
        ],
        compiler_params=pltpu.CompilerParams(
            collective_id=0, has_side_effects=True, vmem_limit_bytes=60 * 1024 * 1024
        ),
    )(
        timestep,
        latent,
        modulation[0].transpose(1, 0, 2),
        qkv_weight[0].transpose(1, 0, 2).reshape(3, ZS, YS, WIDTH, HEAD_DIM),
        out_weight[0].transpose(1, 0),
        stale_kv[0],
    )
    return hidden[None], caches[None]


def solution(mesh):
    placed = (
        P(None, "seq"),
        P(),
        P("section", "cfg", None, None),
        P("section", None, None, "seq"),
        P("section", None, "seq"),
        P("section", None, "cfg", "seq"),
    )
    return jax.shard_map(
        on_device,
        mesh=mesh,
        in_specs=placed,
        out_specs=(P("section", "cfg", "seq"), P("section", None, "cfg", "seq")),
        check_vma=False,
    )
```

```python
import jax
import jax.numpy as jnp
from jax import lax
from jax.experimental import pallas as pl
from jax.experimental.pallas import tpu as pltpu
from jax.sharding import PartitionSpec as P

D = 3072
HEAD_DIM = 128
INNER = 2048
PATCHES = 2
PATCH_TOK = 32
TOKENS = 64
WIDTH = 192
ZS = 4
YS = 4
SEQ = 16
LAYERS = 16
GROUP = ZS * HEAD_DIM
WIDE = ZS * WIDTH
EPS_NORM = 1e-06
MESH = pl.DeviceIdType.MESH

FIRST = 5
HOST = (0, 0, 0, 0, 0, 3, 0, 1, 2, 2, 3, 3, 0, 0, 1, 1)
CHUNKS = 3 * YS + 1
CROSS = 10


def host_of(section):
    place = section * 0
    for layer in range(LAYERS):
        if HOST[layer]:
            place = jnp.where(section == layer, HOST[layer], place)
    return place


def kernel(
    t_ref, latent, mod, wq, wo, stale,
    hid_out, kv_out,
    wbuf, wobuf, modbuf, vecs, cache, hb, hwide, att, own, wide, hst, hland, kvland,
    wot, base, shifted,
    ld_sem, h_send, h_recv, a_send, a_recv,
    w_send, w_recv, f_send, f_recv, m_send, m_recv, s_send, s_recv, o_send, o_recv,
):
    sec = lax.axis_index("section")
    me = lax.axis_index("seq")
    cfg = lax.axis_index("cfg")
    zh = me // YS
    y = lax.rem(me, YS)
    place = host_of(sec)
    spread = sec < FIRST
    hosting = (sec >= FIRST) & (zh == place)
    helping = (sec >= FIRST) & (zh != place)
    other = 1 - cfg
    crossed = sec >= CROSS
    branch = jnp.where(crossed, other, cfg)

    def core_at(section):
        return jnp.where(section >= CROSS, 1 - branch, branch)


    def rows(patch):
        return pl.ds(patch * PATCH_TOK, PATCH_TOK)

    def lanes(number, size=HEAD_DIM):
        return pl.ds(pl.multiple_of(number * size, size), size)

    def remote(src, dst, send, recv, device):
        return pltpu.make_async_remote_copy(
            src_ref=src, dst_ref=dst, send_sem=send, recv_sem=recv,
            device_id=device, device_id_type=MESH,
        )

    def greet(device):
        pl.semaphore_signal(barrier, inc=1, device_id=device, device_id_type=MESH)

    def loop(low, high, act):
        def one(j, _):
            act(j)
            return 0

        lax.fori_loop(low, high, one, 0)

    def each_peer(act, with_self):
        for dz in (2, 1, 3, 0):
            loop(
                1 if dz == 0 and not with_self else 0,
                YS,
                lambda j, dz=dz: act(lax.rem(zh + dz, ZS) * YS + lax.rem(y + j, YS)),
            )

    def each_ring(act, with_self):
        for dy in (2, 1, 3, 0) if with_self else (1, 3, 2):
            act(lax.rem(y + dy, YS))

    def each_helper(act):
        loop(1, ZS, lambda j: act(lax.rem(place + j, ZS)))

    loads = [
        pltpu.make_async_copy(mod, modbuf, ld_sem.at[0]),
        pltpu.make_async_copy(stale, cache.at[zh], ld_sem.at[1]),
        pltpu.make_async_copy(latent, own, ld_sem.at[2]),
        pltpu.make_async_copy(
            wo, wobuf.at[pl.ds(pl.multiple_of(zh * WIDTH, WIDTH), WIDTH)], ld_sem.at[3]
        ),
    ]
    for part in range(3):
        for col in range(YS):
            loads.append(
                pltpu.make_async_copy(
                    wq.at[part, :, col],
                    wbuf.at[part * ZS + zh, col],
                    ld_sem.at[4 + part * YS + col],
                )
            )

    @pl.when(jnp.logical_not(helping))
    def _():
        for one in loads[2:]:
            one.start()

        @pl.when(jnp.logical_not(crossed))
        def _():
            for one in loads[:2]:
                one.start()

    barrier = pltpu.get_barrier_semaphore()

    @pl.when(spread)
    def _():
        each_peer(lambda to: greet((sec, to, cfg)), False)

        @pl.when(sec > 0)
        def _():
            loop(0, SEQ, lambda j: greet((sec - 1, j, core_at(sec - 1))))

        greet((sec, me, other))

    @pl.when(hosting)
    def _():
        def helper(z):
            greet((sec, z * YS + y, cfg))
            greet((sec, z * YS + y, other))

        each_helper(helper)
        greet((sec, me, other))
        each_ring(lambda col: greet((sec, place * YS + col, cfg)), False)

        @pl.when(sec == FIRST)
        def _():
            loop(0, SEQ, lambda j: greet((sec - 1, j, core_at(sec - 1))))

        @pl.when(sec > FIRST)
        def _():
            before = host_of(sec - 1) * YS
            loop(0, YS, lambda j: greet((sec - 1, before + j, core_at(sec - 1))))

    @pl.when(helping)
    def _():
        greet((sec, place * YS + y, cfg))
        greet((sec, place * YS + y, other))
        pl.semaphore_wait(barrier, 2)

    @pl.when(sec < FIRST - 1)
    def _():
        pl.semaphore_wait(barrier, SEQ + SEQ)

    @pl.when(sec == FIRST - 1)
    def _():
        pl.semaphore_wait(barrier, SEQ + YS)

    @pl.when(hosting & (sec < LAYERS - 1))
    def _():
        pl.semaphore_wait(barrier, 2 * YS + 2 * (ZS - 1))

    @pl.when(hosting & (sec == LAYERS - 1))
    def _():
        pl.semaphore_wait(barrier, YS + 2 * (ZS - 1))

    def chunk_at(number, half, z):
        if number == CHUNKS - 1:
            return wobuf.at[
                pl.ds(pl.multiple_of(z * WIDTH, WIDTH), WIDTH), lanes(half, INNER // 2)
            ]
        part, col = divmod(number, YS)
        return wbuf.at[part * ZS + z, col, pl.ds(half * 2, 2)]

    def chunk_from(number, half):
        if number == CHUNKS - 1:
            return wo.at[:, lanes(half, INNER // 2)]
        part, col = divmod(number, YS)
        return wq.at[part, pl.ds(half * 2, 2), col]

    def w_copy(number):
        return remote(
            chunk_from(number, cfg), chunk_at(number, cfg, zh),
            w_send.at[number], w_recv.at[zh, number], (sec, place * YS + y, cfg),
        )

    def w_landing(number, z):
        spot = chunk_at(number, cfg, z)
        return remote(
            spot, spot, w_send.at[number], w_recv.at[z, number], (sec, z * YS + y, cfg)
        )

    def swap(number, z, half):
        spot = chunk_at(number, half, z)
        return remote(
            spot, spot, f_send.at[z, number], f_recv.at[z, number], (sec, me, 1 - cfg)
        )

    def m_copy():
        return remote(mod, modbuf, m_send, m_recv, (sec, me, other))

    def s_copy(to, core):
        return remote(
            stale, cache.at[zh], s_send, s_recv.at[zh], (sec, to * YS + y, core)
        )

    def s_landing(z):
        return remote(
            stale, cache.at[z], s_send, s_recv.at[z], (sec, z * YS + y, cfg)
        )

    def o_copy(z, number):
        src = cache.at[z] if number == 2 else hst.at[z, rows(number)]
        dst = kvland if number == 2 else hland.at[rows(number)]
        return remote(
            src, dst, o_send.at[z, number], o_recv.at[number], (sec, z * YS + y, branch)
        )

    def take_back():
        for number in range(3):
            o_copy(zh, number).wait_recv()
        hid_out[...] = hland[...]
        kv_out[...] = kvland[...]

    @pl.when(helping)
    def _():
        s_copy(place, branch).start()
        for number in range(CHUNKS):
            w_copy(number).start()
        for number in range(CHUNKS):
            w_copy(number).wait_send()
        s_copy(place, branch).wait_send()
        take_back()

    @pl.when(jnp.logical_not(helping) & crossed)
    def _():
        m_copy().start()
        s_copy(zh, other).start()

    def own_arrays():
        @pl.when(crossed)
        def _():
            m_copy().wait()
            s_copy(zh, other).wait_send()
            s_landing(zh).wait_recv()

        @pl.when(jnp.logical_not(crossed))
        def _():
            loads[0].wait()
            loads[1].wait()

    def h_copy(patch, section, to):
        return remote(
            own.at[rows(patch)], hb.at[patch, me],
            h_send.at[patch, to], h_recv.at[patch, me],
            (section, to, core_at(section)),
        )

    def h_landing(patch, source):
        return remote(
            own.at[rows(patch)], hb.at[patch, source],
            h_send.at[patch, source], h_recv.at[patch, source], (sec, source, cfg),
        )

    def wide_copy(patch, to, col):
        return remote(
            wide.at[patch], hwide.at[patch, y],
            h_send.at[patch, col], h_recv.at[patch, y], (sec + 1, to * YS + col, core_at(sec + 1)),
        )

    def wide_landing(patch, col):
        return remote(
            wide.at[patch], hwide.at[patch, col],
            h_send.at[patch, col], h_recv.at[patch, col], (sec, col, cfg),
        )

    def a_copy(patch, source, to):
        spot = att.at[patch, source // YS, :, lanes(lax.rem(source, YS))]
        return remote(
            spot, spot, a_send.at[patch, to], a_recv.at[patch, source], (sec, to, cfg)
        )

    def ring_copy(patch, source, to):
        spot = att.at[patch, source]
        return remote(
            spot, spot, a_send.at[patch, to], a_recv.at[patch, source],
            (sec, place * YS + to, cfg),
        )

    def rms(values):
        square = jnp.mean(values * values, axis=-1, keepdims=True)
        return (values * (1.0 / jnp.sqrt(square + EPS_NORM))).astype(jnp.bfloat16)

    def weights(col):
        return jnp.concatenate(
            [wbuf[number, col].reshape(WIDE, HEAD_DIM) for number in range(3 * ZS)], axis=1
        )

    def own_weights(z):
        return jnp.concatenate(
            [wbuf[part * ZS + zh, :, z].reshape(WIDE, HEAD_DIM) for part in range(3)], axis=1
        )

    def column_sums(weights_of):
        which = lax.broadcasted_iota(jnp.int32, (16, WIDE), 0)
        shift_sum = None
        for number in range(YS):
            here = slice(number * WIDE, (number + 1) * WIDE)
            scale = vecs[1, :, here]
            high = scale.astype(jnp.bfloat16).astype(jnp.float32)
            stack = jnp.where(
                which == 0, high,
                jnp.where(which == 1, scale - high, jnp.where(which == 2, vecs[0, :, here], 0.0)),
            )
            sums = jnp.dot(
                stack.astype(jnp.bfloat16), weights_of(number), preferred_element_type=jnp.float32
            )
            size = sums.shape[1]
            base[number, :, :size] = sums[0:1] + sums[1:2]
            shift_sum = sums[2:3] if shift_sum is None else shift_sum + sums[2:3]
        shifted[:, :size] = shift_sum

    def project(order, block_of, weights_of, size):
        total, parts = None, []
        for number in order:
            block = block_of(number)
            middle = jnp.mean(block, axis=-1, keepdims=True)
            block = block - middle
            parts.append((number, middle, jnp.sum(block * block, axis=-1, keepdims=True)))
            term = jnp.dot(
                (block * vecs[1, :, lanes(number, WIDE)]).astype(jnp.bfloat16),
                weights_of(number),
                preferred_element_type=jnp.float32,
            )
            total = term if total is None else total + term
        mean = sum(part[1] for part in parts) * (1.0 / YS)
        spread_of = sum(part[2] + WIDE * (part[1] - mean) ** 2 for part in parts) * (1.0 / D)
        for number, middle, _ in parts:
            total = total + (middle - mean) * base[number, :, :size]
        return total * (1.0 / jnp.sqrt(spread_of + EPS_NORM)) + shifted[:, :size]

    def modulation_rows(ring):
        own_arrays()
        pick = lax.broadcasted_iota(jnp.int32, (8, D), 0) == t_ref[0]
        for part in range(3):
            row = jnp.sum(
                jnp.where(pick, modbuf[part].astype(jnp.float32), 0.0), axis=0, keepdims=True
            )
            if ring:
                row = jnp.concatenate(
                    [
                        row[:, (z * YS + col) * WIDTH : (z * YS + col + 1) * WIDTH]
                        for col in range(YS)
                        for z in range(ZS)
                    ],
                    axis=1,
                )
            vecs[part] = row + 1.0 if part == 1 else row

    def assemble(patch):
        for col in range(YS):
            hwide[patch, col] = jnp.concatenate(
                [hb[patch, z * YS + col].astype(jnp.float32) for z in range(ZS)], axis=1
            ).astype(jnp.bfloat16)

    def attend(patch, heads):
        for z, _, key, value in heads:
            cache[z, 0, rows(patch), :] = rms(key)
            cache[z, 1, rows(patch), :] = value.astype(jnp.bfloat16)
        queries = [rms(head[1]) for head in heads]
        scores = [
            lax.dot_general(
                query, cache[head[0], 0], (((1,), (1,)), ((), ())),
                preferred_element_type=jnp.float32,
            )
            for head, query in zip(heads, queries)
        ]
        exponents = [jnp.exp(score * HEAD_DIM ** (-0.5)) for score in scores]
        sums = [1.0 / jnp.sum(exponent, axis=-1, keepdims=True) for exponent in exponents]
        probs = [(top * below).astype(jnp.bfloat16) for top, below in zip(exponents, sums)]
        attended = [
            jnp.dot(prob, cache[head[0], 1], preferred_element_type=jnp.float32)
            for head, prob in zip(heads, probs)
        ]
        return [block.astype(jnp.bfloat16) for block in attended]

    def finish(z):
        @pl.when(crossed)
        def _():
            for number in range(3):
                o_copy(z, number).start()
            take_back()
            for number in range(3):
                o_copy(z, number).wait_send()

        @pl.when(jnp.logical_not(crossed))
        def _():
            hid_out[...] = hst[z]
            kv_out[...] = cache[z]

    @pl.when(spread)
    def _():
        loads[2].wait()

        @pl.when(sec == 0)
        def _():
            for patch in range(PATCHES):
                each_peer(lambda to: h_copy(patch, sec, to).start(), False)
                hb[patch, me] = own[rows(patch)]

        modulation_rows(False)
        for one in loads[4:]:
            one.wait()
        column_sums(own_weights)

        def front(patch):
            def block_of(z):
                def arrived(col):
                    @pl.when((sec > 0) | (z * YS + col != me))
                    def _():
                        h_landing(patch, z * YS + col).wait_recv()

                loop(0, YS, arrived)
                return jnp.concatenate(
                    [hb[patch, z * YS + col].astype(jnp.float32) for col in range(YS)], axis=1
                )

            projected = project(
                [lax.rem(zh + dz, ZS) for dz in (0, 1, 3, 2)], block_of, own_weights, 3 * HEAD_DIM
            )
            three = [projected[:, part * HEAD_DIM : (part + 1) * HEAD_DIM] for part in range(3)]
            att[patch, zh, :, lanes(y)] = attend(patch, [(zh, *three)])[0]
            each_peer(lambda to: a_copy(patch, me, to).start(), False)

            @pl.when(sec == 0)
            def _():
                each_peer(lambda to: h_copy(patch, sec, to).wait_send(), False)

        def back(patch):
            if patch == 0:
                loads[3].wait()
            mine = vecs[2, :, lanes(zh, WIDE)]
            gate = jnp.zeros((1, WIDTH), jnp.float32)
            for col in range(YS):
                gate = gate + jnp.where(y == col, mine[:, col * WIDTH : (col + 1) * WIDTH], 0.0)
            part = pl.ds(pl.multiple_of(zh * WIDTH, WIDTH), WIDTH)
            update = None
            for dz in (0, 1, 3, 2):
                z = lax.rem(zh + dz, ZS)
                loop(
                    0 if dz else 1,
                    YS,
                    lambda j, z=z: a_copy(
                        patch, z * YS + lax.rem(y + j, YS), z * YS + lax.rem(y + j, YS)
                    ).wait_recv(),
                )
                term = lax.dot_general(
                    att[patch, z], wobuf[part, lanes(z, GROUP)],
                    (((1,), (1,)), ((), ())),
                    preferred_element_type=jnp.float32,
                )
                update = term if update is None else update + term
            result = (hb[patch, me].astype(jnp.float32) + gate * update).astype(jnp.bfloat16)
            own[rows(patch)] = result

            @pl.when(sec < FIRST - 1)
            def _():
                each_peer(lambda to: h_copy(patch, sec + 1, to).start(), True)

            @pl.when(sec == FIRST - 1)
            def _():
                each_ring(
                    lambda col: h_copy(patch, sec + 1, HOST[FIRST] * YS + col).start(), True
                )

            hst[zh, rows(patch), :] = result

        for patch in range(PATCHES):
            front(patch)
        for patch in range(PATCHES):
            back(patch)
        finish(zh)
        for patch in range(PATCHES):
            each_peer(lambda to: a_copy(patch, me, to).wait_send(), False)

            @pl.when(sec < FIRST - 1)
            def _():
                each_peer(lambda to: h_copy(patch, sec + 1, to).wait_send(), True)

            @pl.when(sec == FIRST - 1)
            def _():
                each_ring(
                    lambda col: h_copy(patch, sec + 1, HOST[FIRST] * YS + col).wait_send(), True
                )

    @pl.when(hosting)
    def _():
        modulation_rows(True)
        for one in loads[2:]:
            one.wait()
        for number in range(CHUNKS):
            def relay(z, number=number):
                w_landing(number, z).wait_recv()
                swap(number, z, cfg).start()

            each_helper(relay)
        each_helper(lambda z: s_landing(z).wait_recv())
        for number in range(CHUNKS):
            each_helper(lambda z: swap(number, z, 1 - cfg).wait_recv())
            each_helper(lambda z: swap(number, z, cfg).wait_send())
        after = host_of(sec + 1)

        def turn(j):
            at = lanes(j)
            wot[lanes(lax.rem(j, YS) * ZS + j // YS), :] = wobuf[:, at].T

        loop(0, INNER // HEAD_DIM, turn)

        column_sums(weights)

        def front(patch):
            @pl.when(sec == FIRST)
            def _():
                loop(0, SEQ, lambda j: h_landing(patch, j).wait_recv())
                assemble(patch)

            def block_of(col):
                @pl.when(sec > FIRST)
                def _():
                    wide_landing(patch, col).wait_recv()

                return hwide[patch, col].astype(jnp.float32)

            projected = project(
                [lax.rem(y + dy, YS) for dy in (2, 3, 1, 0)], block_of, weights, 3 * GROUP
            )
            attended = attend(
                patch,
                [
                    (z, *[
                        projected[:, part * GROUP + z * HEAD_DIM : part * GROUP + (z + 1) * HEAD_DIM]
                        for part in range(3)
                    ])
                    for z in range(ZS)
                ],
            )
            att[patch, y] = jnp.concatenate(attended, axis=1)
            each_ring(lambda col: ring_copy(patch, y, col).start(), False)

        def back(patch):
            update = None
            for dy in (0, 3, 1, 2):
                col = lax.rem(y + dy, YS)
                if dy:
                    ring_copy(patch, col, col).wait_recv()
                term = jnp.dot(
                    att[patch, col], wot[lanes(col, GROUP), :],
                    preferred_element_type=jnp.float32,
                )
                update = term if update is None else update + term
            result = hwide[patch, y].astype(jnp.float32) + vecs[2, :, lanes(y, WIDE)] * update
            wide[patch] = result.astype(jnp.bfloat16)

            @pl.when(sec < LAYERS - 1)
            def _():
                each_ring(lambda col: wide_copy(patch, after, col).start(), True)

            for z in range(ZS):
                hst[z, rows(patch)] = result[:, z * WIDTH : (z + 1) * WIDTH].astype(jnp.bfloat16)

            @pl.when(sec == LAYERS - 1)
            def _():
                each_helper(lambda z: o_copy(z, patch).start())

        for patch in range(PATCHES):
            front(patch)

        @pl.when(sec == LAYERS - 1)
        def _():
            each_helper(lambda z: o_copy(z, 2).start())

        for patch in range(PATCHES):
            back(patch)
        for patch in range(PATCHES):
            each_ring(lambda col: ring_copy(patch, y, col).wait_send(), False)

            @pl.when(sec < LAYERS - 1)
            def _():
                each_ring(lambda col: wide_copy(patch, after, col).wait_send(), True)

        @pl.when(sec < LAYERS - 1)
        def _():
            for number in range(3):
                each_helper(lambda z: o_copy(z, number).start())

        for number in range(3):
            each_helper(lambda z: o_copy(z, number).wait_send())
        finish(place)


def on_device(latent, timestep, modulation, qkv_weight, out_weight, stale_kv):
    any_space = pl.BlockSpec(memory_space=pl.ANY)
    in_vmem = pl.BlockSpec(memory_space=pltpu.VMEM)
    bf16 = jnp.bfloat16
    dma = pltpu.SemaphoreType.DMA
    hidden, caches = pl.pallas_call(
        kernel,
        out_shape=(
            jax.ShapeDtypeStruct((TOKENS, WIDTH), bf16),
            jax.ShapeDtypeStruct((2, TOKENS, HEAD_DIM), bf16),
        ),
        in_specs=[pl.BlockSpec(memory_space=pltpu.SMEM)] + [any_space] * 5,
        out_specs=(in_vmem, in_vmem),
        scratch_shapes=[
            pltpu.VMEM((3 * ZS, YS, ZS, WIDTH, HEAD_DIM), bf16),
            pltpu.VMEM((WIDE, INNER), bf16),
            pltpu.VMEM((3, 8, D), bf16),
            pltpu.VMEM((3, 1, D), jnp.float32),
            pltpu.VMEM((ZS, 2, TOKENS, HEAD_DIM), bf16),
            pltpu.VMEM((PATCHES, SEQ, PATCH_TOK, WIDTH), bf16),
            pltpu.VMEM((PATCHES, YS, PATCH_TOK, WIDE), bf16),
            pltpu.VMEM((PATCHES, ZS, PATCH_TOK, YS * HEAD_DIM), bf16),
            pltpu.VMEM((TOKENS, WIDTH), bf16),
            pltpu.VMEM((PATCHES, PATCH_TOK, WIDE), bf16),
            pltpu.VMEM((ZS, TOKENS, WIDTH), bf16),
            pltpu.VMEM((TOKENS, WIDTH), bf16),
            pltpu.VMEM((2, TOKENS, HEAD_DIM), bf16),
            pltpu.VMEM((INNER, WIDE), bf16),
            pltpu.VMEM((YS, 1, 3 * GROUP), jnp.float32),
            pltpu.VMEM((1, 3 * GROUP), jnp.float32),
            dma((16,)),
            dma((PATCHES, SEQ)),
            dma((PATCHES, SEQ)),
            dma((PATCHES, SEQ)),
            dma((PATCHES, SEQ)),
            dma((CHUNKS,)),
            dma((ZS, CHUNKS)),
            dma((ZS, CHUNKS)),
            dma((ZS, CHUNKS)),
            dma,
            dma,
            dma,
            dma((ZS,)),
            dma((ZS, 3)),
            dma((3,)),
        ],
        compiler_params=pltpu.CompilerParams(
            collective_id=0, has_side_effects=True, vmem_limit_bytes=60 * 1024 * 1024
        ),
    )(
        timestep,
        latent,
        modulation[0].transpose(1, 0, 2),
        qkv_weight[0].transpose(1, 0, 2).reshape(3, ZS, YS, WIDTH, HEAD_DIM),
        out_weight[0].transpose(1, 0),
        stale_kv[0],
    )
    return hidden[None], caches[None]


def solution(mesh):
    placed = (
        P(None, "seq"),
        P(),
        P("section", "cfg", None, None),
        P("section", None, None, "seq"),
        P("section", None, "seq"),
        P("section", None, "cfg", "seq"),
    )
    return jax.shard_map(
        on_device,
        mesh=mesh,
        in_specs=placed,
        out_specs=(P("section", "cfg", "seq"), P("section", None, "cfg", "seq")),
        check_vma=False,
    )
```

```python
import jax
import jax.numpy as jnp
from jax import lax
from jax.experimental import pallas as pl
from jax.experimental.pallas import tpu as pltpu
from jax.sharding import PartitionSpec as P

D = 3072
HEAD_DIM = 128
INNER = 2048
PATCHES = 2
PATCH_TOK = 32
TOKENS = 64
WIDTH = 192
ZS = 4
YS = 4
SEQ = 16
LAYERS = 16
GROUP = ZS * HEAD_DIM
WIDE = ZS * WIDTH
EPS_NORM = 1e-06
MESH = pl.DeviceIdType.MESH

FIRST = 5
HOST = (0, 0, 0, 0, 0, 3, 0, 1, 2, 2, 3, 3, 0, 0, 1, 1)
CHUNKS = 3 * YS + 1
CROSS = 10


def host_of(section):
    place = section * 0
    for layer in range(LAYERS):
        if HOST[layer]:
            place = jnp.where(section == layer, HOST[layer], place)
    return place


def kernel(
    t_ref, latent, mod, wq, wo, stale,
    hid_out, kv_out,
    wbuf, wobuf, modbuf, vecs, cache, hb, hwide, att, own, wide, hst, hland, kvland,
    wot, base, shifted,
    ld_sem, h_send, h_recv, a_send, a_recv,
    w_send, w_recv, f_send, f_recv, m_send, m_recv, s_send, s_recv, o_send, o_recv,
):
    sec = lax.axis_index("section")
    me = lax.axis_index("seq")
    cfg = lax.axis_index("cfg")
    zh = me // YS
    y = lax.rem(me, YS)
    place = host_of(sec)
    spread = sec < FIRST
    hosting = (sec >= FIRST) & (zh == place)
    helping = (sec >= FIRST) & (zh != place)
    other = 1 - cfg
    crossed = sec >= CROSS
    branch = jnp.where(crossed, other, cfg)

    def core_at(section):
        return jnp.where(section >= CROSS, 1 - branch, branch)


    def rows(patch):
        return pl.ds(patch * PATCH_TOK, PATCH_TOK)

    def lanes(number, size=HEAD_DIM):
        return pl.ds(pl.multiple_of(number * size, size), size)

    def remote(src, dst, send, recv, device):
        return pltpu.make_async_remote_copy(
            src_ref=src, dst_ref=dst, send_sem=send, recv_sem=recv,
            device_id=device, device_id_type=MESH,
        )

    def greet(device):
        pl.semaphore_signal(barrier, inc=1, device_id=device, device_id_type=MESH)

    def loop(low, high, act):
        def one(j, _):
            act(j)
            return 0

        lax.fori_loop(low, high, one, 0)

    def each_peer(act, with_self):
        for dz in (2, 1, 3, 0):
            loop(
                1 if dz == 0 and not with_self else 0,
                YS,
                lambda j, dz=dz: act(lax.rem(zh + dz, ZS) * YS + lax.rem(y + j, YS)),
            )

    def each_ring(act, with_self):
        for dy in (2, 1, 3, 0) if with_self else (1, 3, 2):
            act(lax.rem(y + dy, YS))

    def each_helper(act):
        loop(1, ZS, lambda j: act(lax.rem(place + j, ZS)))

    loads = [
        pltpu.make_async_copy(mod, modbuf, ld_sem.at[0]),
        pltpu.make_async_copy(stale, cache.at[zh], ld_sem.at[1]),
        pltpu.make_async_copy(latent, own, ld_sem.at[2]),
        pltpu.make_async_copy(
            wo, wobuf.at[pl.ds(pl.multiple_of(zh * WIDTH, WIDTH), WIDTH)], ld_sem.at[3]
        ),
    ]
    for part in range(3):
        for col in range(YS):
            loads.append(
                pltpu.make_async_copy(
                    wq.at[part, :, col],
                    wbuf.at[part * ZS + zh, col],
                    ld_sem.at[4 + part * YS + col],
                )
            )

    @pl.when(jnp.logical_not(helping))
    def _():
        for one in loads[2:]:
            one.start()

        @pl.when(jnp.logical_not(crossed))
        def _():
            for one in loads[:2]:
                one.start()

    barrier = pltpu.get_barrier_semaphore()

    @pl.when(spread)
    def _():
        each_peer(lambda to: greet((sec, to, cfg)), False)

        @pl.when(sec > 0)
        def _():
            loop(0, SEQ, lambda j: greet((sec - 1, j, core_at(sec - 1))))

        greet((sec, me, other))

    @pl.when(hosting)
    def _():
        def helper(z):
            greet((sec, z * YS + y, cfg))
            greet((sec, z * YS + y, other))

        each_helper(helper)
        greet((sec, me, other))
        each_ring(lambda col: greet((sec, place * YS + col, cfg)), False)

        @pl.when(sec == FIRST)
        def _():
            loop(0, SEQ, lambda j: greet((sec - 1, j, core_at(sec - 1))))

        @pl.when(sec > FIRST)
        def _():
            before = host_of(sec - 1) * YS
            loop(0, YS, lambda j: greet((sec - 1, before + j, core_at(sec - 1))))

    @pl.when(helping)
    def _():
        greet((sec, place * YS + y, cfg))
        greet((sec, place * YS + y, other))
        pl.semaphore_wait(barrier, 2)

    @pl.when(sec < FIRST - 1)
    def _():
        pl.semaphore_wait(barrier, SEQ + SEQ)

    @pl.when(sec == FIRST - 1)
    def _():
        pl.semaphore_wait(barrier, SEQ + YS)

    @pl.when(hosting & (sec < LAYERS - 1))
    def _():
        pl.semaphore_wait(barrier, 2 * YS + 2 * (ZS - 1))

    @pl.when(hosting & (sec == LAYERS - 1))
    def _():
        pl.semaphore_wait(barrier, YS + 2 * (ZS - 1))

    def chunk_at(number, half, z):
        if number == CHUNKS - 1:
            return wobuf.at[
                pl.ds(pl.multiple_of(z * WIDTH, WIDTH), WIDTH), lanes(half, INNER // 2)
            ]
        part, col = divmod(number, YS)
        return wbuf.at[part * ZS + z, col, pl.ds(half * 2, 2)]

    def chunk_from(number, half):
        if number == CHUNKS - 1:
            return wo.at[:, lanes(half, INNER // 2)]
        part, col = divmod(number, YS)
        return wq.at[part, pl.ds(half * 2, 2), col]

    def w_copy(number):
        return remote(
            chunk_from(number, cfg), chunk_at(number, cfg, zh),
            w_send.at[number], w_recv.at[zh, number], (sec, place * YS + y, cfg),
        )

    def w_landing(number, z):
        spot = chunk_at(number, cfg, z)
        return remote(
            spot, spot, w_send.at[number], w_recv.at[z, number], (sec, z * YS + y, cfg)
        )

    def swap(number, z, half):
        spot = chunk_at(number, half, z)
        return remote(
            spot, spot, f_send.at[z, number], f_recv.at[z, number], (sec, me, 1 - cfg)
        )

    def m_copy():
        return remote(mod, modbuf, m_send, m_recv, (sec, me, other))

    def s_copy(to, core):
        return remote(
            stale, cache.at[zh], s_send, s_recv.at[zh], (sec, to * YS + y, core)
        )

    def s_landing(z):
        return remote(
            stale, cache.at[z], s_send, s_recv.at[z], (sec, z * YS + y, cfg)
        )

    def o_copy(z, number):
        src = cache.at[z] if number == 2 else hst.at[z, rows(number)]
        dst = kvland if number == 2 else hland.at[rows(number)]
        return remote(
            src, dst, o_send.at[z, number], o_recv.at[number], (sec, z * YS + y, branch)
        )

    def take_back():
        for number in range(3):
            o_copy(zh, number).wait_recv()
        hid_out[...] = hland[...]
        kv_out[...] = kvland[...]

    @pl.when(helping)
    def _():
        s_copy(place, branch).start()
        for number in range(CHUNKS):
            w_copy(number).start()
        for number in range(CHUNKS):
            w_copy(number).wait_send()
        s_copy(place, branch).wait_send()
        take_back()

    @pl.when(jnp.logical_not(helping) & crossed)
    def _():
        m_copy().start()
        s_copy(zh, other).start()

    def own_arrays():
        @pl.when(crossed)
        def _():
            m_copy().wait()
            s_copy(zh, other).wait_send()
            s_landing(zh).wait_recv()

        @pl.when(jnp.logical_not(crossed))
        def _():
            loads[0].wait()
            loads[1].wait()

    def h_copy(patch, section, to):
        return remote(
            own.at[rows(patch)], hb.at[patch, me],
            h_send.at[patch, to], h_recv.at[patch, me],
            (section, to, core_at(section)),
        )

    def h_landing(patch, source):
        return remote(
            own.at[rows(patch)], hb.at[patch, source],
            h_send.at[patch, source], h_recv.at[patch, source], (sec, source, cfg),
        )

    def wide_copy(patch, to, col):
        return remote(
            wide.at[patch], hwide.at[patch, y],
            h_send.at[patch, col], h_recv.at[patch, y], (sec + 1, to * YS + col, core_at(sec + 1)),
        )

    def wide_landing(patch, col):
        return remote(
            wide.at[patch], hwide.at[patch, col],
            h_send.at[patch, col], h_recv.at[patch, col], (sec, col, cfg),
        )

    def a_copy(patch, source, to):
        spot = att.at[patch, source // YS, :, lanes(lax.rem(source, YS))]
        return remote(
            spot, spot, a_send.at[patch, to], a_recv.at[patch, source], (sec, to, cfg)
        )

    def ring_copy(patch, source, to):
        spot = att.at[patch, source]
        return remote(
            spot, spot, a_send.at[patch, to], a_recv.at[patch, source],
            (sec, place * YS + to, cfg),
        )

    def rms(values):
        square = jnp.mean(values * values, axis=-1, keepdims=True)
        return (values * (1.0 / jnp.sqrt(square + EPS_NORM))).astype(jnp.bfloat16)

    def weights(col):
        return jnp.concatenate(
            [wbuf[number, col].reshape(WIDE, HEAD_DIM) for number in range(3 * ZS)], axis=1
        )

    def own_weights(z):
        return jnp.concatenate(
            [wbuf[part * ZS + zh, :, z].reshape(WIDE, HEAD_DIM) for part in range(3)], axis=1
        )

    def column_sums(weights_of):
        which = lax.broadcasted_iota(jnp.int32, (16, WIDE), 0)
        shift_sum = None
        for number in range(YS):
            here = slice(number * WIDE, (number + 1) * WIDE)
            scale = vecs[1, :, here]
            high = scale.astype(jnp.bfloat16).astype(jnp.float32)
            stack = jnp.where(
                which == 0, high,
                jnp.where(which == 1, scale - high, jnp.where(which == 2, vecs[0, :, here], 0.0)),
            )
            sums = jnp.dot(
                stack.astype(jnp.bfloat16), weights_of(number), preferred_element_type=jnp.float32
            )
            size = sums.shape[1]
            base[number, :, :size] = sums[0:1] + sums[1:2]
            shift_sum = sums[2:3] if shift_sum is None else shift_sum + sums[2:3]
        shifted[:, :size] = shift_sum

    def project(order, block_of, weights_of, size):
        total, parts = None, []
        for number in order:
            block = block_of(number)
            middle = jnp.mean(block, axis=-1, keepdims=True)
            block = block - middle
            parts.append((number, middle, jnp.sum(block * block, axis=-1, keepdims=True)))
            term = jnp.dot(
                (block * vecs[1, :, lanes(number, WIDE)]).astype(jnp.bfloat16),
                weights_of(number),
                preferred_element_type=jnp.float32,
            )
            total = term if total is None else total + term
        mean = sum(part[1] for part in parts) * (1.0 / YS)
        spread_of = sum(part[2] + WIDE * (part[1] - mean) ** 2 for part in parts) * (1.0 / D)
        for number, middle, _ in parts:
            total = total + (middle - mean) * base[number, :, :size]
        return total * (1.0 / jnp.sqrt(spread_of + EPS_NORM)) + shifted[:, :size]

    def modulation_rows(ring):
        own_arrays()
        pick = lax.broadcasted_iota(jnp.int32, (8, D), 0) == t_ref[0]
        for part in range(3):
            row = jnp.sum(
                jnp.where(pick, modbuf[part].astype(jnp.float32), 0.0), axis=0, keepdims=True
            )
            if ring:
                row = jnp.concatenate(
                    [
                        row[:, (z * YS + col) * WIDTH : (z * YS + col + 1) * WIDTH]
                        for col in range(YS)
                        for z in range(ZS)
                    ],
                    axis=1,
                )
            vecs[part] = row + 1.0 if part == 1 else row

    def assemble(patch):
        for col in range(YS):
            hwide[patch, col] = jnp.concatenate(
                [hb[patch, z * YS + col].astype(jnp.float32) for z in range(ZS)], axis=1
            ).astype(jnp.bfloat16)

    def attend(patch, heads):
        for z, _, key, value in heads:
            cache[z, 0, rows(patch), :] = rms(key)
            cache[z, 1, rows(patch), :] = value.astype(jnp.bfloat16)
        queries = [rms(head[1]) for head in heads]
        scores = [
            lax.dot_general(
                query, cache[head[0], 0], (((1,), (1,)), ((), ())),
                preferred_element_type=jnp.float32,
            )
            for head, query in zip(heads, queries)
        ]
        exponents = [jnp.exp(score * HEAD_DIM ** (-0.5)) for score in scores]
        sums = [1.0 / jnp.sum(exponent, axis=-1, keepdims=True) for exponent in exponents]
        probs = [(top * below).astype(jnp.bfloat16) for top, below in zip(exponents, sums)]
        attended = [
            jnp.dot(prob, cache[head[0], 1], preferred_element_type=jnp.float32)
            for head, prob in zip(heads, probs)
        ]
        return [block.astype(jnp.bfloat16) for block in attended]

    def finish(z):
        @pl.when(crossed)
        def _():
            for number in range(3):
                o_copy(z, number).start()
            take_back()
            for number in range(3):
                o_copy(z, number).wait_send()

        @pl.when(jnp.logical_not(crossed))
        def _():
            hid_out[...] = hst[z]
            kv_out[...] = cache[z]

    @pl.when(spread)
    def _():
        loads[2].wait()

        @pl.when(sec == 0)
        def _():
            for patch in range(PATCHES):
                each_peer(lambda to: h_copy(patch, sec, to).start(), False)
                hb[patch, me] = own[rows(patch)]

        modulation_rows(False)
        for one in loads[4:]:
            one.wait()
        column_sums(own_weights)

        def front(patch):
            def block_of(z):
                def arrived(col):
                    @pl.when((sec > 0) | (z * YS + col != me))
                    def _():
                        h_landing(patch, z * YS + col).wait_recv()

                loop(0, YS, arrived)
                return jnp.concatenate(
                    [hb[patch, z * YS + col].astype(jnp.float32) for col in range(YS)], axis=1
                )

            projected = project(
                [lax.rem(zh + dz, ZS) for dz in (0, 1, 3, 2)], block_of, own_weights, 3 * HEAD_DIM
            )
            three = [projected[:, part * HEAD_DIM : (part + 1) * HEAD_DIM] for part in range(3)]
            att[patch, zh, :, lanes(y)] = attend(patch, [(zh, *three)])[0]
            each_peer(lambda to: a_copy(patch, me, to).start(), False)

            @pl.when(sec == 0)
            def _():
                each_peer(lambda to: h_copy(patch, sec, to).wait_send(), False)

        def back(patch):
            if patch == 0:
                loads[3].wait()
            mine = vecs[2, :, lanes(zh, WIDE)]
            gate = jnp.zeros((1, WIDTH), jnp.float32)
            for col in range(YS):
                gate = gate + jnp.where(y == col, mine[:, col * WIDTH : (col + 1) * WIDTH], 0.0)
            part = pl.ds(pl.multiple_of(zh * WIDTH, WIDTH), WIDTH)
            update = None
            for dz in (0, 1, 3, 2):
                z = lax.rem(zh + dz, ZS)
                loop(
                    0 if dz else 1,
                    YS,
                    lambda j, z=z: a_copy(
                        patch, z * YS + lax.rem(y + j, YS), z * YS + lax.rem(y + j, YS)
                    ).wait_recv(),
                )
                term = lax.dot_general(
                    att[patch, z], wobuf[part, lanes(z, GROUP)],
                    (((1,), (1,)), ((), ())),
                    preferred_element_type=jnp.float32,
                )
                update = term if update is None else update + term
            result = (hb[patch, me].astype(jnp.float32) + gate * update).astype(jnp.bfloat16)
            own[rows(patch)] = result

            @pl.when(sec < FIRST - 1)
            def _():
                each_peer(lambda to: h_copy(patch, sec + 1, to).start(), True)

            @pl.when(sec == FIRST - 1)
            def _():
                each_ring(
                    lambda col: h_copy(patch, sec + 1, HOST[FIRST] * YS + col).start(), True
                )

            hst[zh, rows(patch), :] = result

        for patch in range(PATCHES):
            front(patch)
        for patch in range(PATCHES):
            back(patch)
        finish(zh)
        for patch in range(PATCHES):
            each_peer(lambda to: a_copy(patch, me, to).wait_send(), False)

            @pl.when(sec < FIRST - 1)
            def _():
                each_peer(lambda to: h_copy(patch, sec + 1, to).wait_send(), True)

            @pl.when(sec == FIRST - 1)
            def _():
                each_ring(
                    lambda col: h_copy(patch, sec + 1, HOST[FIRST] * YS + col).wait_send(), True
                )

    @pl.when(hosting)
    def _():
        modulation_rows(True)
        for one in loads[2:]:
            one.wait()
        for number in range(CHUNKS):
            def relay(z, number=number):
                w_landing(number, z).wait_recv()
                swap(number, z, cfg).start()

            each_helper(relay)
        each_helper(lambda z: s_landing(z).wait_recv())
        for number in range(CHUNKS):
            each_helper(lambda z: swap(number, z, 1 - cfg).wait_recv())
            each_helper(lambda z: swap(number, z, cfg).wait_send())
        after = host_of(sec + 1)

        def turn(j):
            at = lanes(j)
            wot[lanes(lax.rem(j, YS) * ZS + j // YS), :] = wobuf[:, at].T

        loop(0, INNER // HEAD_DIM, turn)

        column_sums(weights)

        def front(patch):
            @pl.when(sec == FIRST)
            def _():
                loop(0, SEQ, lambda j: h_landing(patch, j).wait_recv())
                assemble(patch)

            def block_of(col):
                @pl.when(sec > FIRST)
                def _():
                    wide_landing(patch, col).wait_recv()

                return hwide[patch, col].astype(jnp.float32)

            projected = project(
                [lax.rem(y + dy, YS) for dy in (2, 3, 1, 0)], block_of, weights, 3 * GROUP
            )
            attended = attend(
                patch,
                [
                    (z, *[
                        projected[:, part * GROUP + z * HEAD_DIM : part * GROUP + (z + 1) * HEAD_DIM]
                        for part in range(3)
                    ])
                    for z in range(ZS)
                ],
            )
            att[patch, y] = jnp.concatenate(attended, axis=1)
            each_ring(lambda col: ring_copy(patch, y, col).start(), False)

        def back(patch):
            update = None
            for dy in (0, 3, 1, 2):
                col = lax.rem(y + dy, YS)
                if dy:
                    ring_copy(patch, col, col).wait_recv()
                term = jnp.dot(
                    att[patch, col], wot[lanes(col, GROUP), :],
                    preferred_element_type=jnp.float32,
                )
                update = term if update is None else update + term
            result = hwide[patch, y].astype(jnp.float32) + vecs[2, :, lanes(y, WIDE)] * update
            wide[patch] = result.astype(jnp.bfloat16)

            @pl.when(sec < LAYERS - 1)
            def _():
                each_ring(lambda col: wide_copy(patch, after, col).start(), True)

            for z in range(ZS):
                hst[z, rows(patch)] = result[:, z * WIDTH : (z + 1) * WIDTH].astype(jnp.bfloat16)

            @pl.when(sec == LAYERS - 1)
            def _():
                for dz in (2, 1, 3):
                    o_copy(lax.rem(place + dz, ZS), patch).start()

        for patch in range(PATCHES):
            front(patch)

        @pl.when(sec == LAYERS - 1)
        def _():
            for dz in (2, 1, 3):
                o_copy(lax.rem(place + dz, ZS), 2).start()

        for patch in range(PATCHES):
            back(patch)
        for patch in range(PATCHES):
            each_ring(lambda col: ring_copy(patch, y, col).wait_send(), False)

            @pl.when(sec < LAYERS - 1)
            def _():
                each_ring(lambda col: wide_copy(patch, after, col).wait_send(), True)

        @pl.when(sec < LAYERS - 1)
        def _():
            for number in range(3):
                each_helper(lambda z: o_copy(z, number).start())

        for number in range(3):
            each_helper(lambda z: o_copy(z, number).wait_send())
        finish(place)


def on_device(latent, timestep, modulation, qkv_weight, out_weight, stale_kv):
    any_space = pl.BlockSpec(memory_space=pl.ANY)
    in_vmem = pl.BlockSpec(memory_space=pltpu.VMEM)
    bf16 = jnp.bfloat16
    dma = pltpu.SemaphoreType.DMA
    hidden, caches = pl.pallas_call(
        kernel,
        out_shape=(
            jax.ShapeDtypeStruct((TOKENS, WIDTH), bf16),
            jax.ShapeDtypeStruct((2, TOKENS, HEAD_DIM), bf16),
        ),
        in_specs=[pl.BlockSpec(memory_space=pltpu.SMEM)] + [any_space] * 5,
        out_specs=(in_vmem, in_vmem),
        scratch_shapes=[
            pltpu.VMEM((3 * ZS, YS, ZS, WIDTH, HEAD_DIM), bf16),
            pltpu.VMEM((WIDE, INNER), bf16),
            pltpu.VMEM((3, 8, D), bf16),
            pltpu.VMEM((3, 1, D), jnp.float32),
            pltpu.VMEM((ZS, 2, TOKENS, HEAD_DIM), bf16),
            pltpu.VMEM((PATCHES, SEQ, PATCH_TOK, WIDTH), bf16),
            pltpu.VMEM((PATCHES, YS, PATCH_TOK, WIDE), bf16),
            pltpu.VMEM((PATCHES, ZS, PATCH_TOK, YS * HEAD_DIM), bf16),
            pltpu.VMEM((TOKENS, WIDTH), bf16),
            pltpu.VMEM((PATCHES, PATCH_TOK, WIDE), bf16),
            pltpu.VMEM((ZS, TOKENS, WIDTH), bf16),
            pltpu.VMEM((TOKENS, WIDTH), bf16),
            pltpu.VMEM((2, TOKENS, HEAD_DIM), bf16),
            pltpu.VMEM((INNER, WIDE), bf16),
            pltpu.VMEM((YS, 1, 3 * GROUP), jnp.float32),
            pltpu.VMEM((1, 3 * GROUP), jnp.float32),
            dma((16,)),
            dma((PATCHES, SEQ)),
            dma((PATCHES, SEQ)),
            dma((PATCHES, SEQ)),
            dma((PATCHES, SEQ)),
            dma((CHUNKS,)),
            dma((ZS, CHUNKS)),
            dma((ZS, CHUNKS)),
            dma((ZS, CHUNKS)),
            dma,
            dma,
            dma,
            dma((ZS,)),
            dma((ZS, 3)),
            dma((3,)),
        ],
        compiler_params=pltpu.CompilerParams(
            collective_id=0, has_side_effects=True, vmem_limit_bytes=60 * 1024 * 1024
        ),
    )(
        timestep,
        latent,
        modulation[0].transpose(1, 0, 2),
        qkv_weight[0].transpose(1, 0, 2).reshape(3, ZS, YS, WIDTH, HEAD_DIM),
        out_weight[0].transpose(1, 0),
        stale_kv[0],
    )
    return hidden[None], caches[None]


def solution(mesh):
    placed = (
        P(None, "seq"),
        P(),
        P("section", "cfg", None, None),
        P("section", None, None, "seq"),
        P("section", None, "seq"),
        P("section", None, "cfg", "seq"),
    )
    return jax.shard_map(
        on_device,
        mesh=mesh,
        in_specs=placed,
        out_specs=(P("section", "cfg", "seq"), P("section", None, "cfg", "seq")),
        check_vma=False,
    )
```
